32 devices in a mesh: segment: 8 (over z, x), seq: 4 (over y, core).
Axes of the slice: x: 2, y: 2, z: 4, core: 2. Of those that a mesh axis runs over, the one named last changes fastest.
Arguments:
- projected: bfloat16 [8, 256, 6144], P('segment', 'seq'), may hold values from -128 to 128
- stream_before: bfloat16 [8, 256, 2048], P('segment', 'seq'), may hold values from -3 to 3
- out_weight: bfloat16 [8, 2048, 2048], P('segment', 'seq'), may hold values from -0.25 to 0.25
- proj_weight: bfloat16 [8, 2048, 6144], P('segment', None, 'seq'), may hold values from -0.125 to 0.125
- norm_gain: float32 [8, 2048], P('segment'), may hold values from 0.1 to 1.9
- block_mask: int32 [1, 2, 2], replicated, may hold values from 0 to 1, as said below
- token_order: int32 [256], replicated, may hold values from 0 to 255, each once
Outputs:
- incoming: bfloat16 [8, 256, 2048], P('segment', 'seq')
- next_projected: bfloat16 [8, 256, 6144], P('segment', None, 'seq')
The draws below stay inside these ranges and needn't reach their ends.
Inputs may be any that keep to these rules, and one draw needn't show every extreme that they name: Each query block may always see the key block at its own place in the window (block_mask[w, b, b] = 1).
All inputs are finite; a program needn't handle non-finite values.
Results may differ from the reference program's by a relative error of at most 0.014.
Values may be sent and summed in bfloat16 or wider, within the bound.
No kernel may reach another device: no remote copies, remote signals or barrier semaphores. Data moves between devices by JAX's collectives and lax.ppermute only.
A program may use at most 64 MiB of HBM per device.

```python
import jax
import jax.numpy as jnp
from jax import lax

D = 2048
HEADS = 16
DH = 128
WIN = 256
BLOCK = 128
SECTIONS = 8
TOKENS = 256
NWIN = 1
BPW = 2
N_SEQ = 4


def draw_projected(key, part):
    drawn = jax.random.truncated_normal(key, -6.0, 6.0, (SECTIONS, TOKENS, HEADS, 3, DH), jnp.float32)
    return drawn.reshape(SECTIONS, TOKENS, 3 * HEADS * DH).astype(jnp.bfloat16)


def draw_block_mask(key, part):
    random_bits = jax.random.randint(jax.random.fold_in(key, 5), (NWIN, BPW, BPW), 0, 2)
    rows_index = jnp.arange(BPW, dtype=jnp.int32)[:, None]
    cols_index = jnp.arange(BPW, dtype=jnp.int32)[None, :]
    diagonal = (rows_index == cols_index).astype(jnp.int32)
    return jnp.maximum(random_bits, diagonal[None, :, :]).astype(jnp.int32)


def level_of(key, extent, cuts, smallest, largest):
    factor_of = 1.0
    for axis_at, parts in cuts:
        heights = jax.random.uniform(jax.random.fold_in(jax.random.fold_in(key, 6), axis_at), (parts,), jnp.float32, smallest / len(cuts), largest / len(cuts))
        factor_of = factor_of * jnp.repeat(jnp.exp(heights), extent[axis_at] // parts).reshape((-1,) + (1,) * (len(extent) - 1 - axis_at))
    return factor_of


def bell_draw(own_key, dims, spread, limit, pieces=(), kind=jnp.bfloat16):
    level = level_of(own_key, dims, pieces, -0.22, 0.18) if pieces else 1.0
    entries = jax.random.normal(own_key, dims, jnp.float32) * spread * level
    return jnp.minimum(jnp.maximum(entries, -limit), limit).astype(kind)


def setup_inputs(seed: int = 0) -> dict:
    streams_of = jax.random.split(jax.random.key(seed), 8)
    projected = draw_projected(jax.random.fold_in(streams_of[7], 71), 0)
    stream_before = bell_draw(streams_of[1], (SECTIONS, TOKENS, D), 0.5, 3.0, ((0, 8), (1, 4)))
    out_weight = bell_draw(streams_of[2], (SECTIONS, D, D), (D // 4) ** -0.5, 0.25, ((0, 8), (1, 4)))
    proj_weight = bell_draw(streams_of[3], (SECTIONS, D, 3 * D), D ** -0.5, 0.125, ((0, 8), (2, 4)))
    norm_gain = jnp.clip(1.0 + 0.18 * jax.random.normal(streams_of[4], (SECTIONS, D), jnp.float32), 0.1, 1.9)
    block_mask = draw_block_mask(jax.random.fold_in(streams_of[7], 71), 0)
    token_order = jax.random.permutation(streams_of[6], TOKENS).astype(jnp.int32)
    return dict(projected=projected, stream_before=stream_before, out_weight=out_weight, proj_weight=proj_weight, norm_gain=norm_gain, block_mask=block_mask, token_order=token_order)


def attend_section(projected, token_order, allowed):
    split = projected.reshape(TOKENS, HEADS, 3, DH)[token_order]
    windows = split.reshape(TOKENS // WIN, WIN, HEADS, 3, DH).astype(jnp.float32)
    scores = jnp.einsum('wqhd,wkhd->whqk', windows[:, :, :, 0], windows[:, :, :, 1]) * DH ** (-0.5)
    masked = jnp.where(allowed[:, None], scores, -jnp.inf)
    highest = lax.optimization_barrier(jnp.max(masked, axis=-1, keepdims=True))
    weights = jnp.exp(masked - highest)
    probs = (weights / lax.optimization_barrier(jnp.sum(weights, axis=-1, keepdims=True))).astype(jnp.bfloat16)
    attended = jnp.einsum('whqk,wkhd->wqhd', probs.astype(jnp.float32), windows[:, :, :, 2]).astype(jnp.bfloat16)
    placed = jnp.zeros((TOKENS, HEADS, DH), jnp.bfloat16).at[token_order].set(attended.reshape(TOKENS, HEADS, DH))
    return placed.reshape(TOKENS, HEADS * DH)

def section_layer(inputs, token_order, allowed):
    projected, stream_before, out_weight = inputs
    placed = attend_section(projected, token_order, allowed)
    per_group = HEADS // N_SEQ * DH
    grouped = jnp.transpose(placed.reshape(TOKENS, N_SEQ, per_group), (1, 0, 2))
    weight_groups = out_weight.reshape(N_SEQ, per_group, D)

    def add_group(branch, pair):
        term = jnp.dot(pair[0], pair[1], preferred_element_type=jnp.float32).astype(jnp.bfloat16)
        term = lax.optimization_barrier(term)
        return (branch + term.astype(jnp.float32), None)
    branch, _ = lax.scan(add_group, jnp.zeros((TOKENS, D), jnp.float32), (grouped, weight_groups))
    return (stream_before.astype(jnp.float32) + branch).astype(jnp.bfloat16)

def next_layer(inputs):
    incoming, gain, proj_weight = inputs
    values = incoming.astype(jnp.float32)
    scale = lax.rsqrt(lax.optimization_barrier(jnp.mean(values * values, axis=-1, keepdims=True)) + 1e-06)
    normed = (values * scale * gain[None, :]).astype(jnp.bfloat16)
    return jnp.dot(normed, proj_weight, preferred_element_type=jnp.float32).astype(jnp.bfloat16)

def reference(projected, stream_before, out_weight, proj_weight, norm_gain, block_mask, token_order):
    allowed = jnp.repeat(jnp.repeat(block_mask, BLOCK, axis=1), BLOCK, axis=2) > 0
    stream_after = lax.map(lambda item: section_layer(item, token_order, allowed), (projected, stream_before, out_weight))
    incoming = jnp.roll(stream_after, 1, axis=0)
    next_projected = lax.map(next_layer, (incoming, norm_gain, proj_weight))
    return (incoming, next_projected)
```

```python
import functools

import jax
import jax.numpy as jnp
from jax import lax
from jax.experimental import pallas as pl
from jax.experimental.pallas import tpu as pltpu
from jax.sharding import PartitionSpec as P

HEADS = 16
DH = 128
WIN = 256
BLOCK = 128
NEG = -1e30
VMEM_LIMIT = 48 * 1024 * 1024

VM = pl.BlockSpec(memory_space=pltpu.VMEM)
ANY = pl.BlockSpec(memory_space=pl.ANY)


def swap(x, by):
    size = lax.axis_size("seq")
    return lax.ppermute(x, "seq", [(i, i ^ by) for i in range(size)])


def onward(x):
    size = lax.axis_size("segment")
    return lax.ppermute(x, "segment", [(i, (i + 1) % size) for i in range(size)])


def cut_kernel(n, src, *refs):
    outs, sems = refs[:n], refs[n]
    width = outs[0].shape[1]
    me = lax.axis_index("seq")
    copies = []
    for j in range(n - 1, -1, -1):
        at = pl.multiple_of((me ^ j) * width, 128)
        copies.append(pltpu.make_async_copy(src.at[0, :, pl.ds(at, width)], outs[j], sems.at[j]))
    for c in copies:
        c.start()
    for c in copies:
        c.wait()


def cut(projected, n):
    _, rows, columns = projected.shape
    width = columns // n
    return pl.pallas_call(
        functools.partial(cut_kernel, n),
        out_shape=[jax.ShapeDtypeStruct((rows, width), projected.dtype)] * n,
        in_specs=[ANY],
        out_specs=[VM] * n,
        scratch_shapes=[pltpu.SemaphoreType.DMA((n,))],
        name="cut_slices",
    )(projected)


def attend_kernel(n, lo, hi, *refs):
    blocks, bias, weight, outs = refs[:n], refs[n], refs[n + 1], refs[n + 2 :]
    rows, width = blocks[0].shape
    heads = width // (3 * DH)
    attended = []
    for h in range(heads):
        c = h * 3 * DH
        q = jnp.concatenate([blocks[j][:, c : c + DH] for j in range(lo, hi)], axis=0)
        k = jnp.concatenate([b[:, c + DH : c + 2 * DH] for b in blocks], axis=0)
        v = jnp.concatenate([b[:, c + 2 * DH : c + 3 * DH] for b in blocks], axis=0)
        s = lax.dot_general(q, k, (((1,), (1,)), ((), ())), preferred_element_type=jnp.float32)
        s = s * DH ** (-0.5) + bias[...]
        m = jnp.max(s, axis=-1, keepdims=True)
        e = jnp.exp(s - m)
        p = (e / jnp.sum(e, axis=-1, keepdims=True)).astype(jnp.bfloat16)
        attended.append(jnp.dot(p, v, preferred_element_type=jnp.float32).astype(jnp.bfloat16))
    attended = jnp.concatenate(attended, axis=1)
    term = jnp.dot(attended, weight[0], preferred_element_type=jnp.float32).astype(jnp.bfloat16)
    for j in range(hi - lo):
        outs[j][...] = term[j * rows : (j + 1) * rows]


def attend(blocks, bias, weight, lo, hi):
    n = len(blocks)
    rows, width = blocks[0].shape
    depth = weight.shape[2]
    heads = width // (3 * DH)
    tokens = n * rows
    return pl.pallas_call(
        functools.partial(attend_kernel, n, lo, hi),
        out_shape=[jax.ShapeDtypeStruct((rows, depth), jnp.bfloat16)] * (hi - lo),
        in_specs=[VM] * (n + 2),
        out_specs=[VM] * (hi - lo),
        compiler_params=pltpu.CompilerParams(vmem_limit_bytes=VMEM_LIMIT),
        cost_estimate=pl.CostEstimate(
            flops=2 * (hi - lo) * rows * heads * DH * (2 * tokens + depth),
            bytes_accessed=2 * heads * DH * depth,
            transcendentals=(hi - lo) * rows * tokens * heads,
        ),
        name="attend_project",
    )(*blocks, bias, weight)


def project_kernel(n, *refs):
    xs, gain, weight, out, normed = refs[:n], refs[n], refs[n + 1], refs[n + 2], refs[n + 3]
    rows = xs[0].shape[0]
    me = lax.axis_index("seq")

    @pl.when(pl.program_id(0) == 0)
    def _():
        for j in range(n):
            x = xs[j][...].astype(jnp.float32)
            scale = lax.rsqrt(jnp.mean(x * x, axis=-1, keepdims=True) + 1e-06)
            at = pl.multiple_of((me ^ j) * rows, rows)
            normed[pl.ds(at, rows), :] = (x * scale * gain[...]).astype(jnp.bfloat16)

    out[0] = jnp.dot(normed[...], weight[0], preferred_element_type=jnp.float32).astype(jnp.bfloat16)


def project(xs, gain, weight):
    n = len(xs)
    rows, depth = xs[0].shape
    width = weight.shape[2]
    tile = 256 if width % 256 == 0 else 128
    return pl.pallas_call(
        functools.partial(project_kernel, n),
        grid=(width // tile,),
        out_shape=jax.ShapeDtypeStruct((1, n * rows, width), jnp.bfloat16),
        in_specs=[VM] * n + [VM, pl.BlockSpec((1, depth, tile), lambda i: (0, 0, i))],
        out_specs=pl.BlockSpec((1, n * rows, tile), lambda i: (0, 0, i)),
        scratch_shapes=[pltpu.VMEM((n * rows, depth), jnp.bfloat16)],
        compiler_params=pltpu.CompilerParams(vmem_limit_bytes=VMEM_LIMIT),
        cost_estimate=pl.CostEstimate(
            flops=2 * n * rows * depth * width, bytes_accessed=2 * depth * width, transcendentals=0
        ),
        name="norm_project",
    )(*xs, gain, weight)


def mask_bias(block_mask, token_order, n, rows):
    tokens = n * rows
    per = block_mask.shape[1]
    count = tokens // BLOCK
    me = lax.axis_index("seq")
    order = jnp.arange(n, dtype=jnp.int32) ^ me
    token = (order[:, None] * rows + jnp.arange(rows, dtype=jnp.int32)[None, :]).reshape(tokens)
    block = jnp.arange(tokens, dtype=jnp.int32) // BLOCK
    own = jnp.sum(jnp.where(token_order[None, :] == token[:, None], block[None, :], 0), axis=1)
    hot = own[:, None] == jnp.arange(count, dtype=jnp.int32)[None, :]
    at = jnp.arange(count)
    full = jnp.where(
        at[:, None] // per == at[None, :] // per,
        jnp.tile(block_mask, (1, 1, count // per)).reshape(count, count),
        0,
    )
    hot = hot.astype(jnp.float32)
    seen = hot @ full.astype(jnp.float32) @ hot.T
    return jnp.where(seen > 0.5, 0.0, NEG)


def local(projected, stream_before, out_weight, proj_weight, norm_gain, block_mask, token_order):
    n = lax.axis_size("seq")
    rows = projected.shape[1]
    cuts = cut(projected, n)
    far = [swap(cuts[j], j) for j in range(n - 1, 1, -1)][::-1]
    blocks = [cuts[0], swap(cuts[1], 1)] + far
    bias = mask_bias(block_mask, token_order, n, rows)
    terms = attend(blocks, bias[2 * rows :], out_weight, 2, n)
    arrived = []
    for k in range(0, n - 2, 2):
        joined = terms[k].astype(jnp.float32) + swap(terms[k + 1], 1).astype(jnp.float32)
        arrived.append(swap(joined.astype(jnp.bfloat16), k + 2))
    near = attend(blocks, bias[: 2 * rows], out_weight, 0, 2)
    total = stream_before[0].astype(jnp.float32) + near[0].astype(jnp.float32) + swap(near[1], 1).astype(jnp.float32)
    for a in arrived:
        total = total + a.astype(jnp.float32)
    incoming = onward(total.astype(jnp.bfloat16))
    xs = [incoming, swap(incoming, 1)]
    for k in range(2, n, 2):
        other = swap(incoming, k)
        xs += [other, swap(other, 1)]
    following = project(xs, norm_gain, proj_weight)
    return (incoming[None], following)


def solution(mesh):
    placed = (
        P("segment", "seq", None),
        P("segment", "seq", None),
        P("segment", "seq", None),
        P("segment", None, "seq"),
        P("segment", None),
        P(),
        P(),
    )
    return jax.shard_map(
        local,
        mesh=mesh,
        in_specs=placed,
        out_specs=(P("segment", "seq", None), P("segment", None, "seq")),
        check_vma=False,
    )
```

```python
import functools

import jax
import jax.numpy as jnp
from jax import lax
from jax.experimental import pallas as pl
from jax.experimental.pallas import tpu as pltpu
from jax.sharding import PartitionSpec as P

HEADS = 16
DH = 128
WIN = 256
BLOCK = 128
NEG = -1e30
VMEM_LIMIT = 48 * 1024 * 1024

VM = pl.BlockSpec(memory_space=pltpu.VMEM)
ANY = pl.BlockSpec(memory_space=pltpu.HBM)


def swap(x, by):
    size = lax.axis_size("seq")
    return lax.ppermute(x, "seq", [(i, i ^ by) for i in range(size)])


def onward(x):
    size = lax.axis_size("segment")
    return lax.ppermute(x, "segment", [(i, (i + 1) % size) for i in range(size)])


def cut_kernel(js, src, *refs):
    outs, sems = refs[: len(js)], refs[len(js)]
    width = outs[0].shape[1]
    me = lax.axis_index("seq")
    copies = []
    for at, j in enumerate(js):
        first = pl.multiple_of((me ^ j) * width, 128)
        copies.append(pltpu.make_async_copy(src.at[0, :, pl.ds(first, width)], outs[at], sems.at[at]))
    for c in copies:
        c.start()
    for c in copies:
        c.wait()


def cut(projected, n, js):
    _, rows, columns = projected.shape
    width = columns // n
    return pl.pallas_call(
        functools.partial(cut_kernel, js),
        out_shape=[jax.ShapeDtypeStruct((rows, width), projected.dtype)] * len(js),
        in_specs=[ANY],
        out_specs=[VM] * len(js),
        scratch_shapes=[pltpu.SemaphoreType.DMA((len(js),))],
        name="cut_slices",
    )(projected)


def load_kernel(pieces, *refs):
    count = len(pieces)
    ins, outs, sems = refs[:count], refs[count : 2 * count], refs[2 * count]
    copies = []
    for i, many in enumerate(pieces):
        step = ins[i].shape[1] // many
        for p in range(many):
            part = (slice(None), pl.ds(p * step, step))
            copies.append(pltpu.make_async_copy(ins[i].at[part], outs[i].at[part], sems.at[len(copies)]))
    for c in copies:
        c.start()
    for c in copies:
        c.wait()


def load(arrays, pieces):
    return pl.pallas_call(
        functools.partial(load_kernel, pieces),
        out_shape=[jax.ShapeDtypeStruct(a.shape, a.dtype) for a in arrays],
        in_specs=[ANY] * len(arrays),
        out_specs=[VM] * len(arrays),
        scratch_shapes=[pltpu.SemaphoreType.DMA((sum(pieces),))],
        compiler_params=pltpu.CompilerParams(vmem_limit_bytes=VMEM_LIMIT),
        cost_estimate=pl.CostEstimate(
            flops=0, bytes_accessed=2 * sum(a.size * a.dtype.itemsize for a in arrays), transcendentals=0
        ),
        name="load_weights",
    )(*arrays)


def attend_kernel(n, lo, hi, *refs):
    blocks, bias, weight, outs = refs[:n], refs[n], refs[n + 1], refs[n + 2 :]
    rows, width = blocks[0].shape
    heads = width // (3 * DH)
    attended = []
    for h in range(heads):
        c = h * 3 * DH
        q = jnp.concatenate([blocks[j][:, c : c + DH] for j in range(lo, hi)], axis=0)
        k = jnp.concatenate([b[:, c + DH : c + 2 * DH] for b in blocks], axis=0)
        v = jnp.concatenate([b[:, c + 2 * DH : c + 3 * DH] for b in blocks], axis=0)
        s = lax.dot_general(q, k, (((1,), (1,)), ((), ())), preferred_element_type=jnp.float32)
        s = s * DH ** (-0.5) + bias[...]
        m = jnp.max(s, axis=-1, keepdims=True)
        e = jnp.exp(s - m)
        p = (e / jnp.sum(e, axis=-1, keepdims=True)).astype(jnp.bfloat16)
        attended.append(jnp.dot(p, v, preferred_element_type=jnp.float32).astype(jnp.bfloat16))
    attended = jnp.concatenate(attended, axis=1)
    term = jnp.dot(attended, weight[0], preferred_element_type=jnp.float32).astype(jnp.bfloat16)
    for j in range(hi - lo):
        outs[j][...] = term[j * rows : (j + 1) * rows]


def attend(blocks, bias, weight, lo):
    hi = lo + 1
    n = len(blocks)
    rows, width = blocks[0].shape
    depth = weight.shape[2]
    heads = width // (3 * DH)
    tokens = n * rows
    return pl.pallas_call(
        functools.partial(attend_kernel, n, lo, hi),
        out_shape=[jax.ShapeDtypeStruct((rows, depth), jnp.bfloat16)] * (hi - lo),
        in_specs=[VM] * (n + 2),
        out_specs=[VM] * (hi - lo),
        compiler_params=pltpu.CompilerParams(vmem_limit_bytes=VMEM_LIMIT),
        cost_estimate=pl.CostEstimate(
            flops=2 * (hi - lo) * rows * heads * DH * (2 * tokens + depth),
            bytes_accessed=2 * heads * DH * depth,
            transcendentals=(hi - lo) * rows * tokens * heads,
        ),
        name="attend_project",
    )(*blocks, bias, weight)


def project_kernel(n, tile, xs, gain, weight, kept, out, normed, made, sems):
    rows = xs[0].shape[0]
    width = weight.shape[2]
    me = lax.axis_index("seq")
    keep = pltpu.make_async_copy(xs[0], kept.at[0], sems.at[0])
    keep.start()
    for j in range(n):
        x = xs[j][...].astype(jnp.float32)
        scale = lax.rsqrt(jnp.mean(x * x, axis=-1, keepdims=True) + 1e-06)
        at = pl.multiple_of((me ^ j) * rows, rows)
        normed[pl.ds(at, rows), :] = (x * scale * gain[...]).astype(jnp.bfloat16)
    copies = [keep]
    for i in range(width // tile):
        part = pl.ds(i * tile, tile)
        made[:, part] = jnp.dot(normed[...], weight[0, :, part], preferred_element_type=jnp.float32).astype(jnp.bfloat16)
        copies.append(pltpu.make_async_copy(made.at[:, part], out.at[0, :, part], sems.at[1 + i]))
        copies[-1].start()
    for c in copies:
        c.wait()


def project(xs, gain, weight):
    n = len(xs)
    rows, depth = xs[0].shape
    width = weight.shape[2]
    tile = 256 if width % 256 == 0 else 128
    return pl.pallas_call(
        functools.partial(project_whole, n, tile),
        out_shape=[
            jax.ShapeDtypeStruct((1, rows, depth), jnp.bfloat16),
            jax.ShapeDtypeStruct((1, n * rows, width), jnp.bfloat16),
        ],
        in_specs=[VM] * (n + 2),
        out_specs=[ANY, ANY],
        scratch_shapes=[
            pltpu.VMEM((n * rows, depth), jnp.bfloat16),
            pltpu.VMEM((n * rows, width), jnp.bfloat16),
            pltpu.SemaphoreType.DMA((1 + width // tile,)),
        ],
        compiler_params=pltpu.CompilerParams(vmem_limit_bytes=VMEM_LIMIT),
        cost_estimate=pl.CostEstimate(
            flops=2 * n * rows * depth * width, bytes_accessed=2 * depth * width, transcendentals=0
        ),
        name="norm_project",
    )(*xs, gain, weight)


def project_whole(n, tile, *refs):
    project_kernel(n, tile, refs[:n], *refs[n:])


def mask_bias(block_mask, token_order, n, rows):
    tokens = n * rows
    per = block_mask.shape[1]
    count = tokens // BLOCK
    me = lax.axis_index("seq")
    order = jnp.arange(n, dtype=jnp.int32) ^ me
    token = (order[:, None] * rows + jnp.arange(rows, dtype=jnp.int32)[None, :]).reshape(tokens)
    block = jnp.arange(tokens, dtype=jnp.int32) // BLOCK
    own = jnp.sum(jnp.where(token_order[None, :] == token[:, None], block[None, :], 0), axis=1)
    hot = own[:, None] == jnp.arange(count, dtype=jnp.int32)[None, :]
    at = jnp.arange(count)
    full = jnp.where(
        at[:, None] // per == at[None, :] // per,
        jnp.tile(block_mask, (1, 1, count // per)).reshape(count, count),
        0,
    )
    hot = hot.astype(jnp.float32)
    seen = hot @ full.astype(jnp.float32) @ hot.T
    return jnp.where(seen > 0.5, 0.0, NEG)


def local(projected, stream_before, out_weight, proj_weight, norm_gain, block_mask, token_order):
    n = lax.axis_size("seq")
    rows = projected.shape[1]
    far_cut = cut(projected, n, tuple(range(2, n)))
    far = [swap(far_cut[j - 2], j) for j in range(2, n)]
    near_cut = cut(projected, n, (0, 1))
    blocks = [near_cut[0], swap(near_cut[1], 1)] + far
    bias = mask_bias(block_mask, token_order, n, rows)
    stream, out_weight, proj_weight = load((stream_before, out_weight, proj_weight), (1, 4, 8))
    sums = []
    for k in range(2, n, 2):
        (crossing,) = attend(blocks, bias[(k + 1) * rows : (k + 2) * rows], out_weight, k + 1)
        (staying,) = attend(blocks, bias[k * rows : (k + 1) * rows], out_weight, k)
        joined = staying.astype(jnp.float32) + swap(crossing, 1).astype(jnp.float32)
        sums.append(joined.astype(jnp.bfloat16))
    arrived = [swap(x, 2 * k + 2) for k, x in enumerate(sums)]
    sums, near_bias = lax.optimization_barrier((sums, bias[: 2 * rows]))
    (crossing,) = attend(blocks, near_bias[rows:], out_weight, 1)
    (staying,) = attend(blocks, near_bias[:rows], out_weight, 0)
    total = stream[0].astype(jnp.float32) + staying.astype(jnp.float32) + swap(crossing, 1).astype(jnp.float32)
    for a in arrived:
        total = total + a.astype(jnp.float32)
    incoming = onward(total.astype(jnp.bfloat16))
    xs = [incoming, swap(incoming, 1)]
    for k in range(2, n, 2):
        other = swap(incoming, k)
        xs += [other, swap(other, 1)]
    kept, following = project(xs, norm_gain, proj_weight)
    return (kept, following)


def solution(mesh):
    placed = (
        P("segment", "seq", None),
        P("segment", "seq", None),
        P("segment", "seq", None),
        P("segment", None, "seq"),
        P("segment", None),
        P(),
        P(),
    )
    return jax.shard_map(
        local,
        mesh=mesh,
        in_specs=placed,
        out_specs=(P("segment", "seq", None), P("segment", None, "seq")),
        check_vma=False,
    )
```

```python
import functools

import jax
import jax.numpy as jnp
from jax import lax
from jax.experimental import pallas as pl
from jax.experimental.pallas import tpu as pltpu
from jax.sharding import PartitionSpec as P

HEADS = 16
DH = 128
WIN = 256
BLOCK = 128
NEG = -1e30
VMEM_LIMIT = 16 * 1024 * 1024
SMALL_LIMIT = 4 * 1024 * 1024

VM = pl.BlockSpec(memory_space=pltpu.VMEM)
ANY = pl.BlockSpec(memory_space=pltpu.HBM)


def swap(x, by):
    size = lax.axis_size("seq")
    return lax.ppermute(x, "seq", [(i, i ^ by) for i in range(size)])


def onward(x):
    size = lax.axis_size("segment")
    return lax.ppermute(x, "segment", [(i, (i + 1) % size) for i in range(size)])


def cut_kernel(js, src, *refs):
    outs, sems = refs[-1 - len(js) : -1], refs[-1]
    width = outs[0].shape[1]
    me = lax.axis_index("seq")
    copies = []
    for at, j in enumerate(js):
        first = pl.multiple_of((me ^ j) * width, 128)
        copies.append(pltpu.make_async_copy(src.at[0, :, pl.ds(first, width)], outs[at], sems.at[at]))
    for c in copies:
        c.start()
    for c in copies:
        c.wait()


def cut(projected, n, js, after=()):
    _, rows, columns = projected.shape
    width = columns // n
    return pl.pallas_call(
        functools.partial(cut_kernel, js),
        out_shape=[jax.ShapeDtypeStruct((rows, width), projected.dtype)] * len(js),
        in_specs=[ANY] * (1 + len(after)),
        out_specs=[VM] * len(js),
        scratch_shapes=[pltpu.SemaphoreType.DMA((len(js),))],
        compiler_params=pltpu.CompilerParams(vmem_limit_bytes=SMALL_LIMIT),
        name="cut_slices",
    )(projected, *after)


def load_kernel(pieces, *refs):
    count = len(pieces)
    ins, outs, sems = refs[:count], refs[-1 - count : -1], refs[-1]
    copies = []
    for i, many in enumerate(pieces):
        step = ins[i].shape[1] // many
        for p in range(many):
            part = (slice(None), pl.ds(p * step, step))
            copies.append(pltpu.make_async_copy(ins[i].at[part], outs[i].at[part], sems.at[len(copies)]))
    for c in copies:
        c.start()
    for c in copies:
        c.wait()


def load(arrays, pieces, after=()):
    return pl.pallas_call(
        functools.partial(load_kernel, pieces),
        out_shape=[jax.ShapeDtypeStruct(a.shape, a.dtype) for a in arrays],
        in_specs=[ANY] * (len(arrays) + len(after)),
        out_specs=[VM] * len(arrays),
        scratch_shapes=[pltpu.SemaphoreType.DMA((sum(pieces),))],
        compiler_params=pltpu.CompilerParams(vmem_limit_bytes=SMALL_LIMIT),
        cost_estimate=pl.CostEstimate(
            flops=0, bytes_accessed=2 * sum(a.size * a.dtype.itemsize for a in arrays), transcendentals=0
        ),
        name="load_weights",
    )(*arrays, *after)


def attend_kernel(n, lo, hi, *refs):
    blocks, bias, weight, outs = refs[:n], refs[n], refs[n + 1], refs[n + 2 :]
    rows, width = blocks[0].shape
    heads = width // (3 * DH)
    attended = []
    for h in range(heads):
        c = h * 3 * DH
        q = jnp.concatenate([blocks[j][:, c : c + DH] for j in range(lo, hi)], axis=0)
        k = jnp.concatenate([b[:, c + DH : c + 2 * DH] for b in blocks], axis=0)
        v = jnp.concatenate([b[:, c + 2 * DH : c + 3 * DH] for b in blocks], axis=0)
        s = lax.dot_general(q, k, (((1,), (1,)), ((), ())), preferred_element_type=jnp.float32)
        s = s * DH ** (-0.5) + bias[...]
        m = jnp.max(s, axis=-1, keepdims=True)
        e = jnp.exp(s - m)
        p = (e / jnp.sum(e, axis=-1, keepdims=True)).astype(jnp.bfloat16)
        attended.append(jnp.dot(p, v, preferred_element_type=jnp.float32).astype(jnp.bfloat16))
    attended = jnp.concatenate(attended, axis=1)
    term = jnp.dot(attended, weight[0], preferred_element_type=jnp.float32).astype(jnp.bfloat16)
    for j in range(hi - lo):
        outs[j][...] = term[j * rows : (j + 1) * rows]


def attend(blocks, bias, weight, lo, hi):
    n = len(blocks)
    rows, width = blocks[0].shape
    depth = weight.shape[2]
    heads = width // (3 * DH)
    tokens = n * rows
    return pl.pallas_call(
        functools.partial(attend_kernel, n, lo, hi),
        out_shape=[jax.ShapeDtypeStruct((rows, depth), jnp.bfloat16)] * (hi - lo),
        in_specs=[VM] * (n + 2),
        out_specs=[VM] * (hi - lo),
        compiler_params=pltpu.CompilerParams(vmem_limit_bytes=VMEM_LIMIT),
        cost_estimate=pl.CostEstimate(
            flops=2 * (hi - lo) * rows * heads * DH * (2 * tokens + depth),
            bytes_accessed=2 * heads * DH * depth,
            transcendentals=(hi - lo) * rows * tokens * heads,
        ),
        name="attend_project",
    )(*blocks, bias, weight)


def project_kernel(n, tile, xs, gain, weight, kept, out, normed, made, sems):
    rows = xs[0].shape[0]
    width = weight.shape[2]
    me = lax.axis_index("seq")
    keep = pltpu.make_async_copy(xs[0], kept.at[0], sems.at[0])
    keep.start()
    for j in range(n):
        x = xs[j][...].astype(jnp.float32)
        scale = lax.rsqrt(jnp.mean(x * x, axis=-1, keepdims=True) + 1e-06)
        at = pl.multiple_of((me ^ j) * rows, rows)
        normed[pl.ds(at, rows), :] = (x * scale * gain[...]).astype(jnp.bfloat16)
    copies = [keep]
    for i in range(width // tile):
        part = pl.ds(i * tile, tile)
        made[:, part] = jnp.dot(normed[...], weight[0, :, part], preferred_element_type=jnp.float32).astype(jnp.bfloat16)
        copies.append(pltpu.make_async_copy(made.at[:, part], out.at[0, :, part], sems.at[1 + i]))
        copies[-1].start()
    for c in copies:
        c.wait()


def project(xs, gain, weight):
    n = len(xs)
    rows, depth = xs[0].shape
    width = weight.shape[2]
    tile = 256 if width % 256 == 0 else 128
    return pl.pallas_call(
        functools.partial(project_whole, n, tile),
        out_shape=[
            jax.ShapeDtypeStruct((1, rows, depth), jnp.bfloat16),
            jax.ShapeDtypeStruct((1, n * rows, width), jnp.bfloat16),
        ],
        in_specs=[VM] * (n + 2),
        out_specs=[ANY, ANY],
        scratch_shapes=[
            pltpu.VMEM((n * rows, depth), jnp.bfloat16),
            pltpu.VMEM((n * rows, width), jnp.bfloat16),
            pltpu.SemaphoreType.DMA((1 + width // tile,)),
        ],
        compiler_params=pltpu.CompilerParams(vmem_limit_bytes=VMEM_LIMIT),
        cost_estimate=pl.CostEstimate(
            flops=2 * n * rows * depth * width, bytes_accessed=2 * depth * width, transcendentals=0
        ),
        name="norm_project",
    )(*xs, gain, weight)


def project_whole(n, tile, *refs):
    project_kernel(n, tile, refs[:n], *refs[n:])


def mask_bias(block_mask, token_order, n, rows):
    tokens = n * rows
    per = block_mask.shape[1]
    count = tokens // BLOCK
    me = lax.axis_index("seq")
    order = jnp.arange(n, dtype=jnp.int32) ^ me
    token = (order[:, None] * rows + jnp.arange(rows, dtype=jnp.int32)[None, :]).reshape(tokens)
    block = jnp.arange(tokens, dtype=jnp.int32) // BLOCK
    own = jnp.sum(jnp.where(token_order[None, :] == token[:, None], block[None, :], 0), axis=1)
    hot = own[:, None] == jnp.arange(count, dtype=jnp.int32)[None, :]
    at = jnp.arange(count)
    full = jnp.where(
        at[:, None] // per == at[None, :] // per,
        jnp.tile(block_mask, (1, 1, count // per)).reshape(count, count),
        0,
    )
    hot = hot.astype(jnp.float32)
    seen = hot @ full.astype(jnp.float32) @ hot.T
    return jnp.where(seen > 0.5, 0.0, NEG)


def local(projected, stream_before, out_weight, proj_weight, norm_gain, block_mask, token_order):
    n = lax.axis_size("seq")
    rows = projected.shape[1]
    far_cut = cut(projected, n, tuple(range(2, n)))
    far = [swap(far_cut[j - 2], j) for j in range(2, n)]
    near_cut = cut(projected, n, (0, 1), (far_cut[0],))
    blocks = [near_cut[0], swap(near_cut[1], 1)] + far
    stream, out_weight = load((stream_before, out_weight), (1, 4))
    bias = mask_bias(block_mask, token_order, n, rows)
    terms = attend(blocks, bias[2 * rows :], out_weight, 2, n)
    sums = []
    for k in range(0, n - 2, 2):
        joined = terms[k].astype(jnp.float32) + swap(terms[k + 1], 1).astype(jnp.float32)
        sums.append(joined.astype(jnp.bfloat16))
    arrived = [swap(x, 2 * k + 2) for k, x in enumerate(sums)]
    staying, crossing = attend(blocks, bias[: 2 * rows], out_weight, 0, 2)
    (proj_weight,) = load((proj_weight,), (8,), (staying,))
    total = stream[0].astype(jnp.float32) + staying.astype(jnp.float32) + swap(crossing, 1).astype(jnp.float32)
    for a in arrived:
        total = total + a.astype(jnp.float32)
    total, proj_weight = lax.optimization_barrier((total.astype(jnp.bfloat16), proj_weight))
    incoming = onward(total)
    xs = [incoming, swap(incoming, 1)]
    for k in range(2, n, 2):
        other = swap(incoming, k)
        xs += [other, swap(other, 1)]
    kept, following = project(xs, norm_gain, proj_weight)
    return (kept, following)


def solution(mesh):
    placed = (
        P("segment", "seq", None),
        P("segment", "seq", None),
        P("segment", "seq", None),
        P("segment", None, "seq"),
        P("segment", None),
        P(),
        P(),
    )
    return jax.shard_map(
        local,
        mesh=mesh,
        in_specs=placed,
        out_specs=(P("segment", "seq", None), P("segment", None, "seq")),
        check_vma=False,
    )
```

```python
import functools

import jax
import jax.numpy as jnp
from jax import lax
from jax.experimental import pallas as pl
from jax.experimental.pallas import tpu as pltpu
from jax.sharding import PartitionSpec as P

HEADS = 16
DH = 128
WIN = 256
BLOCK = 128
NEG = -1e30
VMEM_LIMIT = 16 * 1024 * 1024
SMALL_LIMIT = 4 * 1024 * 1024

VM = pl.BlockSpec(memory_space=pltpu.VMEM)
ANY = pl.BlockSpec(memory_space=pltpu.HBM)


def swap(x, by):
    size = lax.axis_size("seq")
    return lax.ppermute(x, "seq", [(i, i ^ by) for i in range(size)])


def onward(x, by):
    sections, size = lax.axis_size("segment"), lax.axis_size("seq")
    pairs = [
        (s * size + t, (s + 1) % sections * size + (t ^ by)) for s in range(sections) for t in range(size)
    ]
    return lax.ppermute(x, ("segment", "seq"), pairs)


def cut_kernel(js, src, *refs):
    outs, sems = refs[-1 - len(js) : -1], refs[-1]
    width = outs[0].shape[1]
    me = lax.axis_index("seq")
    copies = []
    for at, j in enumerate(js):
        first = pl.multiple_of((me ^ j) * width, 128)
        copies.append(pltpu.make_async_copy(src.at[0, :, pl.ds(first, width)], outs[at], sems.at[at]))
    for c in copies:
        c.start()
    for c in copies:
        c.wait()


def cut(projected, n, js, after=()):
    _, rows, columns = projected.shape
    width = columns // n
    return pl.pallas_call(
        functools.partial(cut_kernel, js),
        out_shape=[jax.ShapeDtypeStruct((rows, width), projected.dtype)] * len(js),
        in_specs=[ANY] * (1 + len(after)),
        out_specs=[VM] * len(js),
        scratch_shapes=[pltpu.SemaphoreType.DMA((len(js),))],
        compiler_params=pltpu.CompilerParams(vmem_limit_bytes=SMALL_LIMIT),
        name="cut_slices",
    )(projected, *after)


def load_kernel(pieces, *refs):
    count = len(pieces)
    ins, outs, sems = refs[:count], refs[-1 - count : -1], refs[-1]
    copies = []
    for i, many in enumerate(pieces):
        step = ins[i].shape[1] // many
        for p in range(many):
            part = (slice(None), pl.ds(p * step, step))
            copies.append(pltpu.make_async_copy(ins[i].at[part], outs[i].at[part], sems.at[len(copies)]))
    for c in copies:
        c.start()
    for c in copies:
        c.wait()


def load(arrays, pieces, after=()):
    return pl.pallas_call(
        functools.partial(load_kernel, pieces),
        out_shape=[jax.ShapeDtypeStruct(a.shape, a.dtype) for a in arrays],
        in_specs=[ANY] * (len(arrays) + len(after)),
        out_specs=[VM] * len(arrays),
        scratch_shapes=[pltpu.SemaphoreType.DMA((sum(pieces),))],
        compiler_params=pltpu.CompilerParams(vmem_limit_bytes=SMALL_LIMIT),
        cost_estimate=pl.CostEstimate(
            flops=0, bytes_accessed=2 * sum(a.size * a.dtype.itemsize for a in arrays), transcendentals=0
        ),
        name="load_weights",
    )(*arrays, *after)


def attend_kernel(n, js, *refs):
    blocks, bias, weight, out = refs[:n], refs[n], refs[n + 1], refs[n + 2]
    rows, width = blocks[0].shape
    heads = width // (3 * DH)
    seen = jnp.concatenate([bias[j * rows : (j + 1) * rows] for j in js], axis=0)
    attended = []
    for h in range(heads):
        c = h * 3 * DH
        q = jnp.concatenate([blocks[j][:, c : c + DH] for j in js], axis=0)
        k = jnp.concatenate([b[:, c + DH : c + 2 * DH] for b in blocks], axis=0)
        v = jnp.concatenate([b[:, c + 2 * DH : c + 3 * DH] for b in blocks], axis=0)
        s = lax.dot_general(q, k, (((1,), (1,)), ((), ())), preferred_element_type=jnp.float32)
        s = s * DH ** (-0.5) + seen
        m = jnp.max(s, axis=-1, keepdims=True)
        e = jnp.exp(s - m)
        p = (e / jnp.sum(e, axis=-1, keepdims=True)).astype(jnp.bfloat16)
        attended.append(jnp.dot(p, v, preferred_element_type=jnp.float32).astype(jnp.bfloat16))
    attended = jnp.concatenate(attended, axis=1)
    out[...] = jnp.dot(attended, weight[0], preferred_element_type=jnp.float32).astype(jnp.bfloat16)


def attend(blocks, bias, weight, js):
    n = len(blocks)
    rows, width = blocks[0].shape
    depth = weight.shape[2]
    heads = width // (3 * DH)
    tokens = n * rows
    return pl.pallas_call(
        functools.partial(attend_kernel, n, js),
        out_shape=jax.ShapeDtypeStruct((len(js) * rows, depth), jnp.bfloat16),
        in_specs=[VM] * (n + 2),
        out_specs=VM,
        compiler_params=pltpu.CompilerParams(vmem_limit_bytes=VMEM_LIMIT),
        cost_estimate=pl.CostEstimate(
            flops=2 * len(js) * rows * heads * DH * (2 * tokens + depth),
            bytes_accessed=2 * heads * DH * depth,
            transcendentals=len(js) * rows * tokens * heads,
        ),
        name="attend_project",
    )(*blocks, bias, weight)


def chip_sum_kernel(rows, cols, mine, theirs, stream, partial, own, *others):
    for i in range(mine.shape[0] // rows):
        part = slice(i * rows, (i + 1) * rows)
        total = mine[part, :].astype(jnp.float32) + theirs[part, :].astype(jnp.float32)
        if i == 0:
            total = total + stream[0].astype(jnp.float32)
            own[...] = total[:, cols:]
        else:
            others[i - 1][...] = total[:, cols:].astype(jnp.bfloat16)
        partial[part, :] = total[:, :cols].astype(jnp.bfloat16)


def chip_sum(mine, theirs, stream, cols):
    rows = stream.shape[1]
    count, depth = mine.shape
    rest = (rows, depth - cols)
    return pl.pallas_call(
        functools.partial(chip_sum_kernel, rows, cols),
        out_shape=[
            jax.ShapeDtypeStruct((count, cols), jnp.bfloat16),
            jax.ShapeDtypeStruct(rest, jnp.float32),
        ]
        + [jax.ShapeDtypeStruct(rest, jnp.bfloat16)] * (count // rows - 1),
        in_specs=[VM] * 3,
        out_specs=[VM] * (count // rows + 1),
        compiler_params=pltpu.CompilerParams(vmem_limit_bytes=SMALL_LIMIT),
        name="chip_sum",
    )(mine, theirs, stream)


def settle_kernel(x, after, out):
    out[...] = x[...]


def settle(x, after):
    return pl.pallas_call(
        settle_kernel,
        out_shape=jax.ShapeDtypeStruct(x.shape, x.dtype),
        in_specs=[VM, ANY],
        out_specs=VM,
        compiler_params=pltpu.CompilerParams(vmem_limit_bytes=SMALL_LIMIT),
        name="settle",
    )(x, after)


def join_kernel(rows, mine, *refs):
    others, out = refs[:-1], refs[-1]
    for i in range(mine.shape[0] // rows):
        total = mine[i * rows : (i + 1) * rows, :].astype(jnp.float32)
        for k, other in enumerate(others):
            at = i ^ (k + 1)
            total = total + other[at * rows : (at + 1) * rows, :].astype(jnp.float32)
        out[i * rows : (i + 1) * rows, :] = total.astype(jnp.bfloat16)


def join(rows, mine, others):
    return pl.pallas_call(
        functools.partial(join_kernel, rows),
        out_shape=jax.ShapeDtypeStruct(mine.shape, mine.dtype),
        in_specs=[VM] * (1 + len(others)),
        out_specs=VM,
        compiler_params=pltpu.CompilerParams(vmem_limit_bytes=SMALL_LIMIT),
        name="join_chips",
    )(mine, *others)


def project_kernel(n, tile, even, odd, *refs):
    rest, gain, weight, kept, out, normed, made, hold, sems = refs[:n], *refs[n:]
    rows, cols = rest[0].shape[0], even.shape[1]
    width = weight.shape[2]
    me = lax.axis_index("seq")
    hold[:, :cols] = even[:rows, :]
    hold[:, cols:] = rest[0][...]
    copies = [pltpu.make_async_copy(hold, kept.at[0], sems.at[0])]
    copies[0].start()
    for j in range(n):
        first = (odd if j % 2 else even)[j // 2 * rows : (j // 2 + 1) * rows, :].astype(jnp.float32)
        second = rest[j][...].astype(jnp.float32)
        squares = jnp.sum(first * first, axis=-1, keepdims=True) + jnp.sum(second * second, axis=-1, keepdims=True)
        scale = lax.rsqrt(squares / normed.shape[1] + 1e-06)
        at = pl.multiple_of((me ^ j) * rows, rows)
        normed[pl.ds(at, rows), :cols] = (first * scale * gain[:, :cols]).astype(jnp.bfloat16)
        normed[pl.ds(at, rows), cols:] = (second * scale * gain[:, cols:]).astype(jnp.bfloat16)
    for i in range(width // tile):
        part = pl.ds(i * tile, tile)
        made[:, part] = jnp.dot(normed[...], weight[0, :, part], preferred_element_type=jnp.float32).astype(jnp.bfloat16)
        copies.append(pltpu.make_async_copy(made.at[:, part], out.at[0, :, part], sems.at[1 + i]))
        copies[-1].start()
    for c in copies:
        c.wait()


def project(even, odd, rest, gain, weight):
    n = len(rest)
    rows = rest[0].shape[0]
    _, depth, width = weight.shape
    tile = 256 if width % 256 == 0 else 128
    return pl.pallas_call(
        functools.partial(project_kernel, n, tile),
        out_shape=[
            jax.ShapeDtypeStruct((1, rows, depth), jnp.bfloat16),
            jax.ShapeDtypeStruct((1, n * rows, width), jnp.bfloat16),
        ],
        in_specs=[VM] * (n + 4),
        out_specs=[ANY, ANY],
        scratch_shapes=[
            pltpu.VMEM((n * rows, depth), jnp.bfloat16),
            pltpu.VMEM((n * rows, width), jnp.bfloat16),
            pltpu.VMEM((rows, depth), jnp.bfloat16),
            pltpu.SemaphoreType.DMA((1 + width // tile,)),
        ],
        compiler_params=pltpu.CompilerParams(vmem_limit_bytes=VMEM_LIMIT),
        cost_estimate=pl.CostEstimate(
            flops=2 * n * rows * depth * width, bytes_accessed=2 * depth * width, transcendentals=0
        ),
        name="norm_project",
    )(even, odd, *rest, gain, weight)


def mask_bias(block_mask, token_order, n, rows):
    tokens = n * rows
    per = block_mask.shape[1]
    count = tokens // BLOCK
    me = lax.axis_index("seq")
    order = jnp.arange(n, dtype=jnp.int32) ^ me
    token = (order[:, None] * rows + jnp.arange(rows, dtype=jnp.int32)[None, :]).reshape(tokens)
    block = jnp.arange(tokens, dtype=jnp.int32) // BLOCK
    own = jnp.sum(jnp.where(token_order[None, :] == token[:, None], block[None, :], 0), axis=1)
    hot = own[:, None] == jnp.arange(count, dtype=jnp.int32)[None, :]
    at = jnp.arange(count)
    full = jnp.where(
        at[:, None] // per == at[None, :] // per,
        jnp.tile(block_mask, (1, 1, count // per)).reshape(count, count),
        0,
    )
    hot = hot.astype(jnp.float32)
    seen = hot @ full.astype(jnp.float32) @ hot.T
    return jnp.where(seen > 0.5, 0.0, NEG)


def local(projected, stream_before, out_weight, proj_weight, norm_gain, block_mask, token_order):
    n = lax.axis_size("seq")
    rows = projected.shape[1]
    far_cut = cut(projected, n, tuple(range(2, n)))
    far = [swap(far_cut[j - 2], j) for j in range(2, n)]
    near_cut = cut(projected, n, (0, 1), (far_cut[0],))
    blocks = [near_cut[0], swap(near_cut[1], 1)] + far
    stream, out_weight = load((stream_before, out_weight), (1, 4))
    bias = mask_bias(block_mask, token_order, n, rows)
    crossing = attend(blocks, bias, out_weight, tuple(range(1, n, 2)))
    staying = attend(blocks, bias, out_weight, tuple(range(0, n, 2)))
    cols = crossing.shape[1] // 2
    partial, own, *others = chip_sum(staying, swap(crossing, 1), stream, cols)
    partial = onward(partial, 0)
    total = own
    for k, x in enumerate(others):
        total = total + swap(x, 2 * k + 2).astype(jnp.float32)
    total = total.astype(jnp.bfloat16)
    rest = [onward(total, j) for j in range(0, n, 2)]
    partial = settle(partial, total)
    swapped = [swap(partial, j) for j in range(2, n, 2)]
    (proj_weight,) = load((proj_weight,), (8,), (partial,))
    rest, proj_weight = lax.optimization_barrier((rest, proj_weight))
    rest = [r for x in rest for r in (x, swap(x, 1))]
    swapped, rest = lax.optimization_barrier((swapped, rest))
    even = join(rows, partial, swapped)
    odd = swap(even, 1)
    kept, following = project(even, odd, rest, norm_gain, proj_weight)
    return (kept, following)


def solution(mesh):
    placed = (
        P("segment", "seq", None),
        P("segment", "seq", None),
        P("segment", "seq", None),
        P("segment", None, "seq"),
        P("segment", None),
        P(),
        P(),
    )
    return jax.shard_map(
        local,
        mesh=mesh,
        in_specs=placed,
        out_specs=(P("segment", "seq", None), P("segment", None, "seq")),
        check_vma=False,
    )
```

```python
import functools
import math

import jax
import jax.numpy as jnp
from jax import lax
from jax.experimental import pallas as pl
from jax.experimental.pallas import tpu as pltpu
from jax.sharding import PartitionSpec as P

HEADS = 16
DH = 128
WIN = 256
BLOCK = 128
NEG = -1e30
VMEM_LIMIT = 16 * 1024 * 1024
SMALL_LIMIT = 4 * 1024 * 1024

VM = pl.BlockSpec(memory_space=pltpu.VMEM)
ANY = pl.BlockSpec(memory_space=pltpu.HBM)


def swap(x, by):
    size = lax.axis_size("seq")
    return lax.ppermute(x, "seq", [(i, i ^ by) for i in range(size)])


def onward(x, by):
    sections, size = lax.axis_size("segment"), lax.axis_size("seq")
    pairs = [
        (s * size + t, (s + 1) % sections * size + (t ^ by)) for s in range(sections) for t in range(size)
    ]
    return lax.ppermute(x, ("segment", "seq"), pairs)


def cut_kernel(js, src, *refs):
    outs, sems = refs[-1 - len(js) : -1], refs[-1]
    width = outs[0].shape[1]
    me = lax.axis_index("seq")
    copies = []
    for at, j in enumerate(js):
        first = pl.multiple_of((me ^ j) * width, 128)
        copies.append(pltpu.make_async_copy(src.at[0, :, pl.ds(first, width)], outs[at], sems.at[at]))
    for c in copies:
        c.start()
    for c in copies:
        c.wait()


def cut(projected, n, js, after=()):
    _, rows, columns = projected.shape
    width = columns // n
    return pl.pallas_call(
        functools.partial(cut_kernel, js),
        out_shape=[pltpu.VMEM((rows, width), projected.dtype)] * len(js),
        in_specs=[ANY] * (1 + len(after)),
        out_specs=[VM] * len(js),
        scratch_shapes=[pltpu.SemaphoreType.DMA((len(js),))],
        compiler_params=pltpu.CompilerParams(vmem_limit_bytes=SMALL_LIMIT),
        name="cut_slices",
    )(pltpu.with_memory_space_constraint(projected, pltpu.HBM), *after)


def load_kernel(pieces, *refs):
    count = len(pieces)
    ins, outs, sems = refs[:count], refs[-1 - count : -1], refs[-1]
    copies = []
    for i, many in enumerate(pieces):
        step = ins[i].shape[1] // many
        for p in range(many):
            part = (slice(None), pl.ds(p * step, step))
            copies.append(pltpu.make_async_copy(ins[i].at[part], outs[i].at[part], sems.at[len(copies)]))
    for c in copies:
        c.start()
    for c in copies:
        c.wait()


def load(arrays, pieces, after=(), cost=0):
    return pl.pallas_call(
        functools.partial(load_kernel, pieces),
        out_shape=[pltpu.VMEM(a.shape, a.dtype) for a in arrays],
        in_specs=[ANY] * (len(arrays) + len(after)),
        out_specs=[VM] * len(arrays),
        scratch_shapes=[pltpu.SemaphoreType.DMA((sum(pieces),))],
        compiler_params=pltpu.CompilerParams(vmem_limit_bytes=SMALL_LIMIT),
        cost_estimate=pl.CostEstimate(
            flops=0, bytes_accessed=cost, transcendentals=0
        ),
        name="load_weights",
    )(*[pltpu.with_memory_space_constraint(a, pltpu.HBM) for a in arrays], *after)


def attention(blocks, bias, js):
    rows, width = blocks[0].shape
    seen = jnp.concatenate([bias[j * rows : (j + 1) * rows] for j in js], axis=0)
    attended = []
    for h in range(width // (3 * DH)):
        c = h * 3 * DH
        q = jnp.concatenate([blocks[j][:, c : c + DH] for j in js], axis=0)
        k = jnp.concatenate([b[:, c + DH : c + 2 * DH] for b in blocks], axis=0)
        v = jnp.concatenate([b[:, c + 2 * DH : c + 3 * DH] for b in blocks], axis=0)
        s = lax.dot_general(q, k, (((1,), (1,)), ((), ())), preferred_element_type=jnp.float32) + seen
        e = jnp.exp2((s - jnp.max(s, axis=-1, keepdims=True)) * (DH ** (-0.5) * math.log2(math.e)))
        mixed = jnp.dot(e.astype(jnp.bfloat16), v, preferred_element_type=jnp.float32)
        attended.append((mixed * (1.0 / jnp.sum(e, axis=-1, keepdims=True))).astype(jnp.bfloat16))
    return jnp.concatenate(attended, axis=1)


def attend_kernel(n, js, *refs):
    blocks, bias, out = refs[:2] + refs[2:n][::-1], refs[n], refs[n + 1]
    out[...] = attention(blocks, bias, js)


def attend_project_kernel(n, js, *refs):
    blocks, bias, weight, out = refs[:2] + refs[2:n][::-1], refs[n], refs[n + 1], refs[n + 2]
    out[...] = jnp.dot(attention(blocks, bias, js), weight[0], preferred_element_type=jnp.float32)


def attend(blocks, bias, js, weight=None):
    n = len(blocks)
    rows, width = blocks[0].shape
    depth = width // 3
    queries = len(js) * rows
    made = (attend_kernel, depth, jnp.bfloat16) if weight is None else (attend_project_kernel, weight.shape[2], jnp.float32)
    return pl.pallas_call(
        functools.partial(made[0], n, js),
        out_shape=jax.ShapeDtypeStruct((queries, made[1]), made[2]),
        in_specs=[VM] * (n + 1 + (weight is not None)),
        out_specs=VM,
        compiler_params=pltpu.CompilerParams(vmem_limit_bytes=VMEM_LIMIT),
        cost_estimate=pl.CostEstimate(
            flops=4 * queries * depth * n * rows + (0 if weight is None else 2 * queries * depth * weight.shape[2]),
            bytes_accessed=2 * n * rows * width,
            transcendentals=queries * n * rows * depth // DH,
        ),
        name="attend" if weight is None else "attend_project",
    )(*blocks[:2], *blocks[2:][::-1], bias, *(() if weight is None else (weight,)))


def chip_sum_kernel(rows, cols, mine, theirs, weight, stream, partial, own, *others):
    total = mine[...] + jnp.dot(theirs[...], weight[0], preferred_element_type=jnp.float32)
    for i in range(mine.shape[0] // rows):
        part = slice(i * rows, (i + 1) * rows)
        here = total[part]
        if i == 0:
            here = here + stream[0].astype(jnp.float32)
            own[...] = here[:, cols:]
        else:
            others[i - 1][...] = here[:, cols:].astype(jnp.bfloat16)
        partial[part, :] = here[:, :cols].astype(jnp.bfloat16)


def chip_sum(mine, theirs, weight, stream, cols):
    rows = stream.shape[1]
    count, depth = mine.shape
    rest = (rows, depth - cols)
    return pl.pallas_call(
        functools.partial(chip_sum_kernel, rows, cols),
        out_shape=[
            jax.ShapeDtypeStruct((count, cols), jnp.bfloat16),
            jax.ShapeDtypeStruct(rest, jnp.float32),
        ]
        + [jax.ShapeDtypeStruct(rest, jnp.bfloat16)] * (count // rows - 1),
        in_specs=[VM] * 4,
        out_specs=[VM] * (count // rows + 1),
        compiler_params=pltpu.CompilerParams(vmem_limit_bytes=VMEM_LIMIT),
        name="chip_sum",
    )(mine, theirs, weight, stream)


def join_kernel(rows, mine, *refs):
    others, out = refs[:-1], refs[-1]
    for i in range(mine.shape[0] // rows):
        total = mine[i * rows : (i + 1) * rows, :].astype(jnp.float32)
        for k, other in enumerate(others):
            at = i ^ (k + 1)
            total = total + other[at * rows : (at + 1) * rows, :].astype(jnp.float32)
        out[i * rows : (i + 1) * rows, :] = total.astype(jnp.bfloat16)


def join(rows, mine, others):
    return pl.pallas_call(
        functools.partial(join_kernel, rows),
        out_shape=jax.ShapeDtypeStruct(mine.shape, mine.dtype),
        in_specs=[VM] * (1 + len(others)),
        out_specs=VM,
        compiler_params=pltpu.CompilerParams(vmem_limit_bytes=SMALL_LIMIT),
        name="join_chips",
    )(mine, *others)


def settle_kernel(x, after, out):
    out[...] = x[...]


def settle(x, after):
    return pl.pallas_call(
        settle_kernel,
        out_shape=jax.ShapeDtypeStruct(x.shape, x.dtype),
        in_specs=[VM, ANY],
        out_specs=VM,
        compiler_params=pltpu.CompilerParams(vmem_limit_bytes=SMALL_LIMIT),
        name="settle",
    )(x, after)


def project_first_kernel(n, *refs):
    rest, gain, weight, total, squares, scaled = refs[:n], *refs[n:]
    rows, count = rest[0].shape
    cols = weight.shape[1] - count
    me = lax.axis_index("seq")
    for j in range(n):
        x = rest[j][...].astype(jnp.float32)
        here = pl.ds(pl.multiple_of((me ^ j) * rows, rows), rows)
        squares[here, :] = jnp.sum(x * x, axis=-1, keepdims=True)
        scaled[here, :] = (x * gain[:, cols:]).astype(jnp.bfloat16)
    total[...] = jnp.dot(scaled[...], weight[0, cols:, :], preferred_element_type=jnp.float32)


def project_first(rest, gain, weight):
    n = len(rest)
    rows, count = rest[0].shape
    width = weight.shape[2]
    tokens = n * rows
    return pl.pallas_call(
        functools.partial(project_first_kernel, n),
        out_shape=[
            jax.ShapeDtypeStruct((tokens, width), jnp.float32),
            jax.ShapeDtypeStruct((tokens, 1), jnp.float32),
        ],
        in_specs=[VM] * (n + 2),
        out_specs=[VM, VM],
        scratch_shapes=[pltpu.VMEM((tokens, count), jnp.bfloat16)],
        compiler_params=pltpu.CompilerParams(vmem_limit_bytes=VMEM_LIMIT),
        cost_estimate=pl.CostEstimate(
            flops=2 * tokens * count * width, bytes_accessed=2 * count * width, transcendentals=0
        ),
        name="project_first",
    )(*rest, gain, weight)


def project_second_kernel(n, tile, even, odd, rest, gain, weight, total, squares, kept, out, scaled, sums, made, sems):
    rows, cols = rest.shape[0], even.shape[1]
    depth, width = weight.shape[1:]
    me = lax.axis_index("seq")
    copies = [
        pltpu.make_async_copy(even.at[:rows], kept.at[0, :, pl.ds(0, cols)], sems.at[0]),
        pltpu.make_async_copy(rest, kept.at[0, :, pl.ds(cols, depth - cols)], sems.at[1]),
    ]
    for c in copies:
        c.start()
    for j in range(n):
        x = (odd if j % 2 else even)[j // 2 * rows : (j // 2 + 1) * rows, :].astype(jnp.float32)
        here = pl.ds(pl.multiple_of((me ^ j) * rows, rows), rows)
        sums[here, :] = squares[here, :] + jnp.sum(x * x, axis=-1, keepdims=True)
        scaled[here, :] = (x * gain[:, :cols]).astype(jnp.bfloat16)
    scale = lax.rsqrt(sums[...] / depth + 1e-06)
    for i in range(width // tile):
        part = pl.ds(i * tile, tile)
        mine = jnp.dot(scaled[...], weight[0, :cols, part], preferred_element_type=jnp.float32)
        made[:, part] = ((total[:, part] + mine) * scale).astype(jnp.bfloat16)
        copies.append(pltpu.make_async_copy(made.at[:, part], out.at[0, :, part], sems.at[2 + i]))
        copies[-1].start()
    for c in copies:
        c.wait()


def project_second(n, even, odd, rest, gain, weight, total, squares):
    rows = rest.shape[0]
    cols = even.shape[1]
    _, depth, width = weight.shape
    tile = 256 if width % 256 == 0 else 128
    return pl.pallas_call(
        functools.partial(project_second_kernel, n, tile),
        out_shape=[
            jax.ShapeDtypeStruct((1, rows, depth), jnp.bfloat16),
            jax.ShapeDtypeStruct((1, n * rows, width), jnp.bfloat16),
        ],
        in_specs=[VM] * 7,
        out_specs=[ANY, ANY],
        scratch_shapes=[
            pltpu.VMEM((n * rows, cols), jnp.bfloat16),
            pltpu.VMEM((n * rows, 1), jnp.float32),
            pltpu.VMEM((n * rows, width), jnp.bfloat16),
            pltpu.SemaphoreType.DMA((2 + width // tile,)),
        ],
        compiler_params=pltpu.CompilerParams(vmem_limit_bytes=VMEM_LIMIT),
        cost_estimate=pl.CostEstimate(
            flops=2 * n * rows * cols * width, bytes_accessed=2 * cols * width, transcendentals=0
        ),
        name="project_second",
    )(even, odd, rest, gain, weight, total, squares)


def mask_kernel(rows, mask, order, out):
    tokens = out.shape[0]
    windows, per, _ = mask.shape
    lanes = max(windows * per, 128)
    me = lax.axis_index("seq")
    row = lax.broadcasted_iota(jnp.int32, (tokens, tokens), 0)
    token = ((row // rows) ^ me) * rows + row % rows
    at = (order[...].reshape(1, tokens) == token).astype(jnp.bfloat16)
    position = lax.broadcasted_iota(jnp.int32, (tokens, lanes), 0)
    lane = lax.broadcasted_iota(jnp.int32, (tokens, lanes), 1)
    block = jnp.dot(
        at, (position // BLOCK == lane).astype(jnp.bfloat16), preferred_element_type=jnp.float32
    ).astype(jnp.bfloat16)
    first = lax.broadcasted_iota(jnp.int32, (lanes, lanes), 0)
    second = lax.broadcasted_iota(jnp.int32, (lanes, lanes), 1)
    visible = jnp.zeros((lanes, lanes), jnp.int32)
    for w in range(windows):
        for i in range(per):
            for j in range(per):
                here = (first == w * per + i) & (second == w * per + j)
                visible = jnp.where(here, mask[w, i, j], visible)
    visible = (visible > 0).astype(jnp.bfloat16)
    reach = jnp.dot(block, visible, preferred_element_type=jnp.float32).astype(jnp.bfloat16)
    seen = lax.dot_general(reach, block, (((1,), (1,)), ((), ())), preferred_element_type=jnp.float32)
    out[...] = jnp.where(seen > 0.5, 0.0, NEG)


def mask_bias(block_mask, token_order, n, rows):
    tokens = n * rows
    return pl.pallas_call(
        functools.partial(mask_kernel, rows),
        out_shape=jax.ShapeDtypeStruct((tokens, tokens), jnp.float32),
        in_specs=[pl.BlockSpec(memory_space=pltpu.SMEM), VM],
        out_specs=VM,
        compiler_params=pltpu.CompilerParams(vmem_limit_bytes=SMALL_LIMIT + 24 * tokens * tokens),
        name="mask_bias",
    )(block_mask, token_order)


def local(projected, stream_before, out_weight, proj_weight, norm_gain, block_mask, token_order):
    n = lax.axis_size("seq")
    rows = projected.shape[1]
    far_cut = cut(projected, n, tuple(range(2, n)))
    far = [swap(far_cut[j - 2], j) for j in range(2, n)]
    near_cut = cut(projected, n, (0, 1), (far_cut[0],))
    blocks = [near_cut[0], swap(near_cut[1], 1)] + far
    beside_weight = swap(out_weight, 1)
    stream, out_weight = load((stream_before, out_weight), (1, 4), (near_cut[0],))
    bias = mask_bias(block_mask, token_order, n, rows)
    bias, out_weight = lax.optimization_barrier((bias, out_weight))
    crossing = attend(blocks, bias, tuple(range(1, n, 2)))
    staying = attend(blocks, bias, tuple(range(0, n, 2)), out_weight)
    cols = out_weight.shape[2] * 7 // 16
    partial, own, *others = chip_sum(staying, swap(crossing, 1), beside_weight, stream, cols)
    partial = onward(partial, 0)
    total = own
    for k, x in enumerate(others):
        total = total + swap(x, 2 * k + 2).astype(jnp.float32)
    total = total.astype(jnp.bfloat16)
    rest = [onward(total, j) for j in range(0, n, 2)]
    partial = settle(partial, total)
    swapped = [swap(partial, j) for j in range(2, n, 2)]
    (proj_weight,) = load((proj_weight,), (8,), (partial,), 2 * proj_weight.size)
    rest, proj_weight = lax.optimization_barrier((rest, proj_weight))
    rest = [r for x in rest for r in (x, swap(x, 1))]
    swapped, rest = lax.optimization_barrier((swapped, rest))
    even = join(rows, partial, swapped)
    odd = swap(even, 1)
    total, squares = project_first(rest, norm_gain, proj_weight)
    kept, following = project_second(n, even, odd, rest[0], norm_gain, proj_weight, total, squares)
    return (kept, following)


def solution(mesh):
    placed = (
        P("segment", "seq", None),
        P("segment", "seq", None),
        P("segment", "seq", None),
        P("segment", None, "seq"),
        P("segment", None),
        P(),
        P(),
    )
    return jax.shard_map(
        local,
        mesh=mesh,
        in_specs=placed,
        out_specs=(P("segment", "seq", None), P("segment", None, "seq")),
        check_vma=False,
    )
```

```python
import functools
import math

import jax
import jax.numpy as jnp
from jax import lax
from jax.experimental import pallas as pl
from jax.experimental.pallas import tpu as pltpu
from jax.sharding import PartitionSpec as P

HEADS = 16
DH = 128
WIN = 256
BLOCK = 128
NEG = -1e30
VMEM_LIMIT = 16 * 1024 * 1024
SMALL_LIMIT = 4 * 1024 * 1024

VM = pl.BlockSpec(memory_space=pltpu.VMEM)
ANY = pl.BlockSpec(memory_space=pltpu.HBM)


def swap(x, by):
    size = lax.axis_size("seq")
    return lax.ppermute(x, "seq", [(i, i ^ by) for i in range(size)])


def onward(x, by):
    sections, size = lax.axis_size("segment"), lax.axis_size("seq")
    pairs = [
        (s * size + t, (s + 1) % sections * size + (t ^ by)) for s in range(sections) for t in range(size)
    ]
    return lax.ppermute(x, ("segment", "seq"), pairs)


def cut_kernel(js, src, *refs):
    outs, sems = refs[-1 - len(js) : -1], refs[-1]
    width = outs[0].shape[1]
    me = lax.axis_index("seq")
    copies = []
    for at, j in enumerate(js):
        first = pl.multiple_of((me ^ j) * width, 128)
        copies.append(pltpu.make_async_copy(src.at[0, :, pl.ds(first, width)], outs[at], sems.at[at]))
    for c in copies:
        c.start()
    for c in copies:
        c.wait()


def cut(projected, n, js, after=()):
    _, rows, columns = projected.shape
    width = columns // n
    return pl.pallas_call(
        functools.partial(cut_kernel, js),
        out_shape=[pltpu.VMEM((rows, width), projected.dtype)] * len(js),
        in_specs=[ANY] * (1 + len(after)),
        out_specs=[VM] * len(js),
        scratch_shapes=[pltpu.SemaphoreType.DMA((len(js),))],
        compiler_params=pltpu.CompilerParams(vmem_limit_bytes=SMALL_LIMIT),
        name="cut_slices",
    )(pltpu.with_memory_space_constraint(projected, pltpu.HBM), *after)


def load_kernel(pieces, *refs):
    count = len(pieces)
    ins, outs, sems = refs[:count], refs[-1 - count : -1], refs[-1]
    copies = []
    for i, many in enumerate(pieces):
        step = ins[i].shape[1] // many
        for p in range(many):
            part = (slice(None), pl.ds(p * step, step))
            copies.append(pltpu.make_async_copy(ins[i].at[part], outs[i].at[part], sems.at[len(copies)]))
    for c in copies:
        c.start()
    for c in copies:
        c.wait()


def load(arrays, pieces, after=()):
    return pl.pallas_call(
        functools.partial(load_kernel, pieces),
        out_shape=[pltpu.VMEM(a.shape, a.dtype) for a in arrays],
        in_specs=[ANY] * (len(arrays) + len(after)),
        out_specs=[VM] * len(arrays),
        scratch_shapes=[pltpu.SemaphoreType.DMA((sum(pieces),))],
        compiler_params=pltpu.CompilerParams(vmem_limit_bytes=SMALL_LIMIT),
        cost_estimate=pl.CostEstimate(
            flops=0, bytes_accessed=2 * sum(a.size * a.dtype.itemsize for a in arrays), transcendentals=0
        ),
        name="load_weights",
    )(*[pltpu.with_memory_space_constraint(a, pltpu.HBM) for a in arrays], *after)


def attention(blocks, bias, js):
    rows, width = blocks[0].shape
    seen = jnp.concatenate([bias[j * rows : (j + 1) * rows] for j in js], axis=0)
    attended = []
    for h in range(width // (3 * DH)):
        c = h * 3 * DH
        q = jnp.concatenate([blocks[j][:, c : c + DH] for j in js], axis=0)
        k = jnp.concatenate([b[:, c + DH : c + 2 * DH] for b in blocks], axis=0)
        v = jnp.concatenate([b[:, c + 2 * DH : c + 3 * DH] for b in blocks], axis=0)
        s = lax.dot_general(q, k, (((1,), (1,)), ((), ())), preferred_element_type=jnp.float32) + seen
        e = jnp.exp2((s - jnp.max(s, axis=-1, keepdims=True)) * (DH ** (-0.5) * math.log2(math.e)))
        mixed = jnp.dot(e.astype(jnp.bfloat16), v, preferred_element_type=jnp.float32)
        attended.append((mixed * (1.0 / jnp.sum(e, axis=-1, keepdims=True))).astype(jnp.bfloat16))
    return jnp.concatenate(attended, axis=1)


def attend_kernel(n, js, *refs):
    blocks, bias, out = refs[:n], refs[n], refs[n + 1]
    out[...] = attention(blocks, bias, js)


def attend_project_kernel(n, js, *refs):
    blocks, bias, weight, out = refs[:n], refs[n], refs[n + 1], refs[n + 2]
    out[...] = jnp.dot(
        attention(blocks, bias, js), weight[0], preferred_element_type=jnp.float32
    ).astype(jnp.bfloat16)


def attend(blocks, bias, js, weight=None):
    n = len(blocks)
    rows, width = blocks[0].shape
    depth = width // 3
    queries = len(js) * rows
    made = (attend_kernel, depth, jnp.bfloat16) if weight is None else (attend_project_kernel, weight.shape[2], jnp.bfloat16)
    return pl.pallas_call(
        functools.partial(made[0], n, js),
        out_shape=jax.ShapeDtypeStruct((queries, made[1]), made[2]),
        in_specs=[VM] * (n + 1 + (weight is not None)),
        out_specs=VM,
        compiler_params=pltpu.CompilerParams(vmem_limit_bytes=VMEM_LIMIT),
        cost_estimate=pl.CostEstimate(
            flops=4 * queries * depth * n * rows + (0 if weight is None else 2 * queries * depth * weight.shape[2]),
            bytes_accessed=2 * n * rows * width,
            transcendentals=queries * n * rows * depth // DH,
        ),
        name="attend" if weight is None else "attend_project",
    )(*blocks, bias, *(() if weight is None else (weight,)))


def chip_sum_kernel(rows, cols, mine, theirs, stream, partial, own, *others):
    for i in range(mine.shape[0] // rows):
        part = slice(i * rows, (i + 1) * rows)
        total = mine[part, :].astype(jnp.float32) + theirs[part, :].astype(jnp.float32)
        if i == 0:
            total = total + stream[0].astype(jnp.float32)
            own[...] = total[:, cols:]
        else:
            others[i - 1][...] = total[:, cols:].astype(jnp.bfloat16)
        partial[part, :] = total[:, :cols].astype(jnp.bfloat16)


def chip_sum(mine, theirs, stream, cols):
    rows = stream.shape[1]
    count, depth = mine.shape
    rest = (rows, depth - cols)
    return pl.pallas_call(
        functools.partial(chip_sum_kernel, rows, cols),
        out_shape=[
            jax.ShapeDtypeStruct((count, cols), jnp.bfloat16),
            jax.ShapeDtypeStruct(rest, jnp.float32),
        ]
        + [jax.ShapeDtypeStruct(rest, jnp.bfloat16)] * (count // rows - 1),
        in_specs=[VM] * 3,
        out_specs=[VM] * (count // rows + 1),
        compiler_params=pltpu.CompilerParams(vmem_limit_bytes=SMALL_LIMIT),
        name="chip_sum",
    )(mine, theirs, stream)


def settle_kernel(x, after, out):
    out[...] = x[...]


def settle(x, after):
    return pl.pallas_call(
        settle_kernel,
        out_shape=jax.ShapeDtypeStruct(x.shape, x.dtype),
        in_specs=[VM, ANY],
        out_specs=VM,
        compiler_params=pltpu.CompilerParams(vmem_limit_bytes=SMALL_LIMIT),
        name="settle",
    )(x, after)


def join_kernel(rows, mine, *refs):
    others, out = refs[:-1], refs[-1]
    for i in range(mine.shape[0] // rows):
        total = mine[i * rows : (i + 1) * rows, :].astype(jnp.float32)
        for k, other in enumerate(others):
            at = i ^ (k + 1)
            total = total + other[at * rows : (at + 1) * rows, :].astype(jnp.float32)
        out[i * rows : (i + 1) * rows, :] = total.astype(jnp.bfloat16)


def join(rows, mine, others):
    return pl.pallas_call(
        functools.partial(join_kernel, rows),
        out_shape=jax.ShapeDtypeStruct(mine.shape, mine.dtype),
        in_specs=[VM] * (1 + len(others)),
        out_specs=VM,
        compiler_params=pltpu.CompilerParams(vmem_limit_bytes=SMALL_LIMIT),
        name="join_chips",
    )(mine, *others)


def project_first_kernel(n, *refs):
    rest, gain, weight, total, squares, scaled = refs[:n], *refs[n:]
    rows, count = rest[0].shape
    cols = weight.shape[1] - count
    me = lax.axis_index("seq")
    for j in range(n):
        x = rest[j][...].astype(jnp.float32)
        here = pl.ds(pl.multiple_of((me ^ j) * rows, rows), rows)
        squares[here, :] = jnp.sum(x * x, axis=-1, keepdims=True)
        scaled[here, :] = (x * gain[:, cols:]).astype(jnp.bfloat16)
    total[...] = jnp.dot(scaled[...], weight[0, cols:, :], preferred_element_type=jnp.float32)


def project_first(rest, gain, weight):
    n = len(rest)
    rows, count = rest[0].shape
    width = weight.shape[2]
    tokens = n * rows
    return pl.pallas_call(
        functools.partial(project_first_kernel, n),
        out_shape=[
            jax.ShapeDtypeStruct((tokens, width), jnp.float32),
            jax.ShapeDtypeStruct((tokens, 1), jnp.float32),
        ],
        in_specs=[VM] * (n + 2),
        out_specs=[VM, VM],
        scratch_shapes=[pltpu.VMEM((tokens, count), jnp.bfloat16)],
        compiler_params=pltpu.CompilerParams(vmem_limit_bytes=VMEM_LIMIT),
        cost_estimate=pl.CostEstimate(
            flops=2 * tokens * count * width, bytes_accessed=2 * count * width, transcendentals=0
        ),
        name="project_first",
    )(*rest, gain, weight)


def project_second_kernel(n, tile, even, odd, rest, gain, weight, total, squares, kept, out, scaled, sums, made, sems):
    rows, cols = rest.shape[0], even.shape[1]
    depth, width = weight.shape[1:]
    me = lax.axis_index("seq")
    copies = [
        pltpu.make_async_copy(even.at[:rows], kept.at[0, :, pl.ds(0, cols)], sems.at[0]),
        pltpu.make_async_copy(rest, kept.at[0, :, pl.ds(cols, depth - cols)], sems.at[1]),
    ]
    for c in copies:
        c.start()
    for j in range(n):
        x = (odd if j % 2 else even)[j // 2 * rows : (j // 2 + 1) * rows, :].astype(jnp.float32)
        here = pl.ds(pl.multiple_of((me ^ j) * rows, rows), rows)
        sums[here, :] = squares[here, :] + jnp.sum(x * x, axis=-1, keepdims=True)
        scaled[here, :] = (x * gain[:, :cols]).astype(jnp.bfloat16)
    scale = lax.rsqrt(sums[...] / depth + 1e-06)
    for i in range(width // tile):
        part = pl.ds(i * tile, tile)
        mine = jnp.dot(scaled[...], weight[0, :cols, part], preferred_element_type=jnp.float32)
        made[:, part] = ((total[:, part] + mine) * scale).astype(jnp.bfloat16)
        copies.append(pltpu.make_async_copy(made.at[:, part], out.at[0, :, part], sems.at[2 + i]))
        copies[-1].start()
    for c in copies:
        c.wait()


def project_second(n, even, odd, rest, gain, weight, total, squares):
    rows = rest.shape[0]
    cols = even.shape[1]
    _, depth, width = weight.shape
    tile = 256 if width % 256 == 0 else 128
    return pl.pallas_call(
        functools.partial(project_second_kernel, n, tile),
        out_shape=[
            jax.ShapeDtypeStruct((1, rows, depth), jnp.bfloat16),
            jax.ShapeDtypeStruct((1, n * rows, width), jnp.bfloat16),
        ],
        in_specs=[VM] * 7,
        out_specs=[ANY, ANY],
        scratch_shapes=[
            pltpu.VMEM((n * rows, cols), jnp.bfloat16),
            pltpu.VMEM((n * rows, 1), jnp.float32),
            pltpu.VMEM((n * rows, width), jnp.bfloat16),
            pltpu.SemaphoreType.DMA((2 + width // tile,)),
        ],
        compiler_params=pltpu.CompilerParams(vmem_limit_bytes=VMEM_LIMIT),
        cost_estimate=pl.CostEstimate(
            flops=2 * n * rows * cols * width, bytes_accessed=2 * cols * width, transcendentals=0
        ),
        name="project_second",
    )(even, odd, rest, gain, weight, total, squares)


def mask_kernel(rows, mask, order, out):
    tokens = out.shape[0]
    windows, per, _ = mask.shape
    lanes = max(windows * per, 128)
    me = lax.axis_index("seq")
    row = lax.broadcasted_iota(jnp.int32, (tokens, tokens), 0)
    token = ((row // rows) ^ me) * rows + row % rows
    at = (order[...].reshape(1, tokens) == token).astype(jnp.bfloat16)
    position = lax.broadcasted_iota(jnp.int32, (tokens, lanes), 0)
    lane = lax.broadcasted_iota(jnp.int32, (tokens, lanes), 1)
    block = jnp.dot(
        at, (position // BLOCK == lane).astype(jnp.bfloat16), preferred_element_type=jnp.float32
    ).astype(jnp.bfloat16)
    first = lax.broadcasted_iota(jnp.int32, (lanes, lanes), 0)
    second = lax.broadcasted_iota(jnp.int32, (lanes, lanes), 1)
    visible = jnp.zeros((lanes, lanes), jnp.int32)
    for w in range(windows):
        for i in range(per):
            for j in range(per):
                here = (first == w * per + i) & (second == w * per + j)
                visible = jnp.where(here, mask[w, i, j], visible)
    visible = (visible > 0).astype(jnp.bfloat16)
    reach = jnp.dot(block, visible, preferred_element_type=jnp.float32).astype(jnp.bfloat16)
    seen = lax.dot_general(reach, block, (((1,), (1,)), ((), ())), preferred_element_type=jnp.float32)
    out[...] = jnp.where(seen > 0.5, 0.0, NEG)


def mask_bias(block_mask, token_order, n, rows):
    tokens = n * rows
    return pl.pallas_call(
        functools.partial(mask_kernel, rows),
        out_shape=jax.ShapeDtypeStruct((tokens, tokens), jnp.float32),
        in_specs=[pl.BlockSpec(memory_space=pltpu.SMEM), VM],
        out_specs=VM,
        compiler_params=pltpu.CompilerParams(vmem_limit_bytes=SMALL_LIMIT + 24 * tokens * tokens),
        name="mask_bias",
    )(block_mask, token_order)


def local(projected, stream_before, out_weight, proj_weight, norm_gain, block_mask, token_order):
    n = lax.axis_size("seq")
    rows = projected.shape[1]
    far_cut = cut(projected, n, tuple(range(2, n)))
    far = [swap(far_cut[j - 2], j) for j in range(2, n)]
    near_cut = cut(projected, n, (0, 1), (far_cut[-1],))
    blocks = [near_cut[0], swap(near_cut[1], 1)] + far
    stream, out_weight = load((stream_before, out_weight), (1, 4))
    bias = mask_bias(block_mask, token_order, n, rows)
    crossing = attend(blocks, bias, tuple(range(1, n, 2)), out_weight)
    staying = attend(blocks, bias, tuple(range(0, n, 2)), out_weight)
    cols = crossing.shape[1] * 7 // 16
    partial, own, *others = chip_sum(staying, swap(crossing, 1), stream, cols)
    partial = onward(partial, 0)
    total = own
    for k, x in enumerate(others):
        total = total + swap(x, 2 * k + 2).astype(jnp.float32)
    total = total.astype(jnp.bfloat16)
    rest = [onward(total, j) for j in range(0, n, 2)]
    partial = settle(partial, total)
    swapped = [swap(partial, j) for j in range(2, n, 2)]
    (proj_weight,) = load((proj_weight,), (8,), (partial,))
    rest, proj_weight = lax.optimization_barrier((rest, proj_weight))
    rest = [r for x in rest for r in (x, swap(x, 1))]
    swapped, rest = lax.optimization_barrier((swapped, rest))
    even = join(rows, partial, swapped)
    odd = swap(even, 1)
    total, squares = project_first(rest, norm_gain, proj_weight)
    kept, following = project_second(n, even, odd, rest[0], norm_gain, proj_weight, total, squares)
    return (kept, following)


def solution(mesh):
    placed = (
        P("segment", "seq", None),
        P("segment", "seq", None),
        P("segment", "seq", None),
        P("segment", None, "seq"),
        P("segment", None),
        P(),
        P(),
    )
    return jax.shard_map(
        local,
        mesh=mesh,
        in_specs=placed,
        out_specs=(P("segment", "seq", None), P("segment", None, "seq")),
        check_vma=False,
    )
```

```python
import functools
import math

import jax
import jax.numpy as jnp
from jax import lax
from jax.experimental import pallas as pl
from jax.experimental.pallas import tpu as pltpu
from jax.sharding import PartitionSpec as P

HEADS = 16
DH = 128
WIN = 256
BLOCK = 128
NEG = -1e30
VMEM_LIMIT = 16 * 1024 * 1024
SMALL_LIMIT = 4 * 1024 * 1024

VM = pl.BlockSpec(memory_space=pltpu.VMEM)
ANY = pl.BlockSpec(memory_space=pltpu.HBM)


def swap(x, by):
    size = lax.axis_size("seq")
    return lax.ppermute(x, "seq", [(i, i ^ by) for i in range(size)])


def onward(x, by):
    sections, size = lax.axis_size("segment"), lax.axis_size("seq")
    pairs = [
        (s * size + t, (s + 1) % sections * size + (t ^ by)) for s in range(sections) for t in range(size)
    ]
    return lax.ppermute(x, ("segment", "seq"), pairs)


def cut_kernel(js, src, *refs):
    outs, sems = refs[-1 - len(js) : -1], refs[-1]
    width = outs[0].shape[1]
    me = lax.axis_index("seq")
    copies = []
    for at, j in enumerate(js):
        first = pl.multiple_of((me ^ j) * width, 128)
        copies.append(pltpu.make_async_copy(src.at[0, :, pl.ds(first, width)], outs[at], sems.at[at]))
    for c in copies:
        c.start()
    for c in copies:
        c.wait()


def cut(projected, n, js, after=()):
    _, rows, columns = projected.shape
    width = columns // n
    return pl.pallas_call(
        functools.partial(cut_kernel, js),
        out_shape=[pltpu.VMEM((rows, width), projected.dtype)] * len(js),
        in_specs=[ANY] * (1 + len(after)),
        out_specs=[VM] * len(js),
        scratch_shapes=[pltpu.SemaphoreType.DMA((len(js),))],
        compiler_params=pltpu.CompilerParams(vmem_limit_bytes=SMALL_LIMIT),
        name="cut_slices",
    )(pltpu.with_memory_space_constraint(projected, pltpu.HBM), *after)


def load_kernel(pieces, *refs):
    count = len(pieces)
    ins, outs, sems = refs[:count], refs[-1 - count : -1], refs[-1]
    copies = []
    for i, many in enumerate(pieces):
        step = ins[i].shape[1] // many
        for p in range(many):
            part = (slice(None), pl.ds(p * step, step))
            copies.append(pltpu.make_async_copy(ins[i].at[part], outs[i].at[part], sems.at[len(copies)]))
    for c in copies:
        c.start()
    for c in copies:
        c.wait()


def load(arrays, pieces, after=()):
    return pl.pallas_call(
        functools.partial(load_kernel, pieces),
        out_shape=[pltpu.VMEM(a.shape, a.dtype) for a in arrays],
        in_specs=[ANY] * (len(arrays) + len(after)),
        out_specs=[VM] * len(arrays),
        scratch_shapes=[pltpu.SemaphoreType.DMA((sum(pieces),))],
        compiler_params=pltpu.CompilerParams(vmem_limit_bytes=SMALL_LIMIT),
        cost_estimate=pl.CostEstimate(
            flops=0, bytes_accessed=2 * sum(a.size * a.dtype.itemsize for a in arrays), transcendentals=0
        ),
        name="load_weights",
    )(*[pltpu.with_memory_space_constraint(a, pltpu.HBM) for a in arrays], *after)


def attention(blocks, bias, js):
    rows, width = blocks[0].shape
    seen = jnp.concatenate([bias[j * rows : (j + 1) * rows] for j in js], axis=0)
    attended = []
    for h in range(width // (3 * DH)):
        c = h * 3 * DH
        q = jnp.concatenate([blocks[j][:, c : c + DH] for j in js], axis=0)
        k = jnp.concatenate([b[:, c + DH : c + 2 * DH] for b in blocks], axis=0)
        v = jnp.concatenate([b[:, c + 2 * DH : c + 3 * DH] for b in blocks], axis=0)
        s = lax.dot_general(q, k, (((1,), (1,)), ((), ())), preferred_element_type=jnp.float32) + seen
        e = jnp.exp2((s - jnp.max(s, axis=-1, keepdims=True)) * (DH ** (-0.5) * math.log2(math.e)))
        mixed = jnp.dot(e.astype(jnp.bfloat16), v, preferred_element_type=jnp.float32)
        attended.append((mixed * (1.0 / jnp.sum(e, axis=-1, keepdims=True))).astype(jnp.bfloat16))
    return jnp.concatenate(attended, axis=1)


def attend_project_kernel(n, js, *refs):
    blocks, bias, weight, near, far = refs[:n], refs[n], refs[n + 1], refs[n + 2], refs[n + 3]
    term = jnp.dot(attention(blocks, bias, js), weight[0], preferred_element_type=jnp.float32).astype(jnp.bfloat16)
    rows = near.shape[0]
    near[...] = term[:rows]
    far[...] = term[rows:]


def attend(blocks, bias, js, weight):
    n = len(blocks)
    rows, width = blocks[0].shape
    depth = weight.shape[2]
    queries = len(js) * rows
    return pl.pallas_call(
        functools.partial(attend_project_kernel, n, js),
        out_shape=[
            jax.ShapeDtypeStruct((rows, depth), jnp.bfloat16),
            jax.ShapeDtypeStruct((queries - rows, depth), jnp.bfloat16),
        ],
        in_specs=[VM] * (n + 2),
        out_specs=[VM, VM],
        compiler_params=pltpu.CompilerParams(vmem_limit_bytes=VMEM_LIMIT),
        cost_estimate=pl.CostEstimate(
            flops=2 * queries * width // 3 * (2 * n * rows + depth),
            bytes_accessed=2 * n * rows * width,
            transcendentals=queries * n * rows * width // (3 * DH),
        ),
        name="attend_project",
    )(*blocks, bias, weight)


def far_sum_kernel(rows, cols, mine, theirs, partial, *others):
    total = mine[...].astype(jnp.float32) + theirs[...].astype(jnp.float32)
    partial[...] = total[:, :cols].astype(jnp.bfloat16)
    for i, other in enumerate(others):
        other[...] = total[i * rows : (i + 1) * rows, cols:].astype(jnp.bfloat16)


def far_sum(mine, theirs, rows, cols):
    count, depth = mine.shape
    return pl.pallas_call(
        functools.partial(far_sum_kernel, rows, cols),
        out_shape=[jax.ShapeDtypeStruct((count, cols), jnp.bfloat16)]
        + [jax.ShapeDtypeStruct((rows, depth - cols), jnp.bfloat16)] * (count // rows),
        in_specs=[VM] * 2,
        out_specs=[VM] * (count // rows + 1),
        compiler_params=pltpu.CompilerParams(vmem_limit_bytes=VMEM_LIMIT),
        name="far_sum",
    )(mine, theirs)


def near_sum_kernel(mine, theirs, stream, far, partial, own):
    rows, cols = mine.shape[0], partial.shape[1]
    total = mine[...].astype(jnp.float32) + theirs[...].astype(jnp.float32) + stream[0].astype(jnp.float32)
    partial[:rows, :] = total[:, :cols].astype(jnp.bfloat16)
    partial[rows:, :] = far[...]
    own[...] = total[:, cols:]


def near_sum(mine, theirs, stream, far):
    rows, depth = mine.shape
    count, cols = far.shape
    return pl.pallas_call(
        near_sum_kernel,
        out_shape=[
            jax.ShapeDtypeStruct((rows + count, cols), jnp.bfloat16),
            jax.ShapeDtypeStruct((rows, depth - cols), jnp.float32),
        ],
        in_specs=[VM] * 4,
        out_specs=[VM] * 2,
        compiler_params=pltpu.CompilerParams(vmem_limit_bytes=SMALL_LIMIT),
        name="near_sum",
    )(mine, theirs, stream, far)


def settle_kernel(x, after, out):
    out[...] = x[...]


def settle(x, after):
    return pl.pallas_call(
        settle_kernel,
        out_shape=jax.ShapeDtypeStruct(x.shape, x.dtype),
        in_specs=[VM, ANY],
        out_specs=VM,
        compiler_params=pltpu.CompilerParams(vmem_limit_bytes=SMALL_LIMIT),
        name="settle",
    )(x, after)


def join_kernel(rows, mine, *refs):
    others, out = refs[:-1], refs[-1]
    for i in range(mine.shape[0] // rows):
        total = mine[i * rows : (i + 1) * rows, :].astype(jnp.float32)
        for k, other in enumerate(others):
            at = i ^ (k + 1)
            total = total + other[at * rows : (at + 1) * rows, :].astype(jnp.float32)
        out[i * rows : (i + 1) * rows, :] = total.astype(jnp.bfloat16)


def join(rows, mine, others):
    return pl.pallas_call(
        functools.partial(join_kernel, rows),
        out_shape=jax.ShapeDtypeStruct(mine.shape, mine.dtype),
        in_specs=[VM] * (1 + len(others)),
        out_specs=VM,
        compiler_params=pltpu.CompilerParams(vmem_limit_bytes=SMALL_LIMIT),
        name="join_chips",
    )(mine, *others)


def project_first_kernel(n, *refs):
    rest, gain, weight, total, squares, scaled = refs[:n], *refs[n:]
    rows, count = rest[0].shape
    cols = weight.shape[1] - count
    me = lax.axis_index("seq")
    for j in range(n):
        x = rest[j][...].astype(jnp.float32)
        here = pl.ds(pl.multiple_of((me ^ j) * rows, rows), rows)
        squares[here, :] = jnp.sum(x * x, axis=-1, keepdims=True)
        scaled[here, :] = (x * gain[:, cols:]).astype(jnp.bfloat16)
    total[...] = jnp.dot(scaled[...], weight[0, cols:, :], preferred_element_type=jnp.float32)


def project_first(rest, gain, weight):
    n = len(rest)
    rows, count = rest[0].shape
    width = weight.shape[2]
    tokens = n * rows
    return pl.pallas_call(
        functools.partial(project_first_kernel, n),
        out_shape=[
            jax.ShapeDtypeStruct((tokens, width), jnp.float32),
            jax.ShapeDtypeStruct((tokens, 1), jnp.float32),
        ],
        in_specs=[VM] * (n + 2),
        out_specs=[VM, VM],
        scratch_shapes=[pltpu.VMEM((tokens, count), jnp.bfloat16)],
        compiler_params=pltpu.CompilerParams(vmem_limit_bytes=VMEM_LIMIT),
        cost_estimate=pl.CostEstimate(
            flops=2 * tokens * count * width, bytes_accessed=2 * count * width, transcendentals=0
        ),
        name="project_first",
    )(*rest, gain, weight)


def project_second_kernel(n, tile, even, odd, rest, gain, weight, total, squares, kept, out, scaled, sums, made, sems):
    rows, cols = rest.shape[0], even.shape[1]
    depth, width = weight.shape[1:]
    me = lax.axis_index("seq")
    copies = [
        pltpu.make_async_copy(even.at[:rows], kept.at[0, :, pl.ds(0, cols)], sems.at[0]),
        pltpu.make_async_copy(rest, kept.at[0, :, pl.ds(cols, depth - cols)], sems.at[1]),
    ]
    for c in copies:
        c.start()
    for j in range(n):
        x = (odd if j % 2 else even)[j // 2 * rows : (j // 2 + 1) * rows, :].astype(jnp.float32)
        here = pl.ds(pl.multiple_of((me ^ j) * rows, rows), rows)
        sums[here, :] = squares[here, :] + jnp.sum(x * x, axis=-1, keepdims=True)
        scaled[here, :] = (x * gain[:, :cols]).astype(jnp.bfloat16)
    scale = lax.rsqrt(sums[...] / depth + 1e-06)
    for i in range(width // tile):
        part = pl.ds(i * tile, tile)
        mine = jnp.dot(scaled[...], weight[0, :cols, part], preferred_element_type=jnp.float32)
        made[:, part] = ((total[:, part] + mine) * scale).astype(jnp.bfloat16)
        copies.append(pltpu.make_async_copy(made.at[:, part], out.at[0, :, part], sems.at[2 + i]))
        copies[-1].start()
    for c in copies:
        c.wait()


def project_second(n, even, odd, rest, gain, weight, total, squares):
    rows = rest.shape[0]
    cols = even.shape[1]
    _, depth, width = weight.shape
    tile = 256 if width % 256 == 0 else 128
    return pl.pallas_call(
        functools.partial(project_second_kernel, n, tile),
        out_shape=[
            jax.ShapeDtypeStruct((1, rows, depth), jnp.bfloat16),
            jax.ShapeDtypeStruct((1, n * rows, width), jnp.bfloat16),
        ],
        in_specs=[VM] * 7,
        out_specs=[ANY, ANY],
        scratch_shapes=[
            pltpu.VMEM((n * rows, cols), jnp.bfloat16),
            pltpu.VMEM((n * rows, 1), jnp.float32),
            pltpu.VMEM((n * rows, width), jnp.bfloat16),
            pltpu.SemaphoreType.DMA((2 + width // tile,)),
        ],
        compiler_params=pltpu.CompilerParams(vmem_limit_bytes=VMEM_LIMIT),
        cost_estimate=pl.CostEstimate(
            flops=2 * n * rows * cols * width, bytes_accessed=2 * cols * width, transcendentals=0
        ),
        name="project_second",
    )(even, odd, rest, gain, weight, total, squares)


def mask_kernel(rows, mask, order, out):
    tokens = out.shape[0]
    windows, per, _ = mask.shape
    lanes = max(windows * per, 128)
    me = lax.axis_index("seq")
    row = lax.broadcasted_iota(jnp.int32, (tokens, tokens), 0)
    token = ((row // rows) ^ me) * rows + row % rows
    at = (order[...].reshape(1, tokens) == token).astype(jnp.bfloat16)
    position = lax.broadcasted_iota(jnp.int32, (tokens, lanes), 0)
    lane = lax.broadcasted_iota(jnp.int32, (tokens, lanes), 1)
    block = jnp.dot(
        at, (position // BLOCK == lane).astype(jnp.bfloat16), preferred_element_type=jnp.float32
    ).astype(jnp.bfloat16)
    first = lax.broadcasted_iota(jnp.int32, (lanes, lanes), 0)
    second = lax.broadcasted_iota(jnp.int32, (lanes, lanes), 1)
    visible = jnp.zeros((lanes, lanes), jnp.int32)
    for w in range(windows):
        for i in range(per):
            for j in range(per):
                here = (first == w * per + i) & (second == w * per + j)
                visible = jnp.where(here, mask[w, i, j], visible)
    visible = (visible > 0).astype(jnp.bfloat16)
    reach = jnp.dot(block, visible, preferred_element_type=jnp.float32).astype(jnp.bfloat16)
    seen = lax.dot_general(reach, block, (((1,), (1,)), ((), ())), preferred_element_type=jnp.float32)
    out[...] = jnp.where(seen > 0.5, 0.0, NEG)


def mask_bias(block_mask, token_order, n, rows):
    tokens = n * rows
    return pl.pallas_call(
        functools.partial(mask_kernel, rows),
        out_shape=jax.ShapeDtypeStruct((tokens, tokens), jnp.float32),
        in_specs=[pl.BlockSpec(memory_space=pltpu.SMEM), VM],
        out_specs=VM,
        compiler_params=pltpu.CompilerParams(vmem_limit_bytes=SMALL_LIMIT + 24 * tokens * tokens),
        name="mask_bias",
    )(block_mask, token_order)


def local(projected, stream_before, out_weight, proj_weight, norm_gain, block_mask, token_order):
    n = lax.axis_size("seq")
    rows = projected.shape[1]
    far_cut = cut(projected, n, tuple(range(2, n)))
    far = [swap(far_cut[j - 2], j) for j in range(2, n)]
    near_cut = cut(projected, n, (0, 1), (far_cut[-1],))
    blocks = [near_cut[0], swap(near_cut[1], 1)] + far
    stream, out_weight = load((stream_before, out_weight), (1, 4))
    bias = mask_bias(block_mask, token_order, n, rows)
    near_out, far_out = attend(blocks, bias, tuple(range(1, n, 2)), out_weight)
    near_own, far_own = attend(blocks, bias, tuple(range(0, n, 2)), out_weight)
    cols = out_weight.shape[2] * 7 // 16
    far_partial, *others = far_sum(far_own, swap(far_out, 1), rows, cols)
    partial, own = near_sum(near_own, swap(near_out, 1), stream, far_partial)
    partial = onward(partial, 0)
    (proj_weight,) = load((proj_weight,), (8,), (own,))
    total, proj_weight = lax.optimization_barrier((own, proj_weight))
    for k, x in enumerate(others):
        total = total + swap(x, 2 * k + 2).astype(jnp.float32)
    total = total.astype(jnp.bfloat16)
    rest = [onward(total, j) for j in range(0, n, 2)]
    partial = settle(partial, total)
    swapped = [swap(partial, j) for j in range(2, n, 2)]
    rest = [r for x in rest for r in (x, swap(x, 1))]
    swapped, rest = lax.optimization_barrier((swapped, rest))
    even = join(rows, partial, swapped)
    odd = swap(even, 1)
    total, squares = project_first(rest, norm_gain, proj_weight)
    kept, following = project_second(n, even, odd, rest[0], norm_gain, proj_weight, total, squares)
    return (kept, following)


def solution(mesh):
    placed = (
        P("segment", "seq", None),
        P("segment", "seq", None),
        P("segment", "seq", None),
        P("segment", None, "seq"),
        P("segment", None),
        P(),
        P(),
    )
    return jax.shard_map(
        local,
        mesh=mesh,
        in_specs=placed,
        out_specs=(P("segment", "seq", None), P("segment", None, "seq")),
        check_vma=False,
    )
```

```python
import functools
import math

import jax
import jax.numpy as jnp
from jax import lax
from jax.experimental import pallas as pl
from jax.experimental.pallas import tpu as pltpu
from jax.sharding import PartitionSpec as P

HEADS = 16
DH = 128
WIN = 256
BLOCK = 128
NEG = -1e30
VMEM_LIMIT = 16 * 1024 * 1024
SMALL_LIMIT = 4 * 1024 * 1024

VM = pl.BlockSpec(memory_space=pltpu.VMEM)
ANY = pl.BlockSpec(memory_space=pltpu.HBM)


def swap(x, by):
    size = lax.axis_size("seq")
    return lax.ppermute(x, "seq", [(i, i ^ by) for i in range(size)])


def onward(x, by):
    sections, size = lax.axis_size("segment"), lax.axis_size("seq")
    pairs = [
        (s * size + t, (s + 1) % sections * size + (t ^ by)) for s in range(sections) for t in range(size)
    ]
    return lax.ppermute(x, ("segment", "seq"), pairs)


def cut_kernel(js, src, *refs):
    outs, sems = refs[-1 - len(js) : -1], refs[-1]
    width = outs[0].shape[1]
    me = lax.axis_index("seq")
    copies = []
    for at, j in enumerate(js):
        first = pl.multiple_of((me ^ j) * width, 128)
        copies.append(pltpu.make_async_copy(src.at[0, :, pl.ds(first, width)], outs[at], sems.at[at]))
    for c in copies:
        c.start()
    for c in copies:
        c.wait()


def cut(projected, n, js, after=()):
    _, rows, columns = projected.shape
    width = columns // n
    return pl.pallas_call(
        functools.partial(cut_kernel, js),
        out_shape=[pltpu.VMEM((rows, width), projected.dtype)] * len(js),
        in_specs=[ANY] * (1 + len(after)),
        out_specs=[VM] * len(js),
        scratch_shapes=[pltpu.SemaphoreType.DMA((len(js),))],
        compiler_params=pltpu.CompilerParams(vmem_limit_bytes=SMALL_LIMIT),
        name="cut_slices",
    )(pltpu.with_memory_space_constraint(projected, pltpu.HBM), *after)


def load_kernel(pieces, *refs):
    count = len(pieces)
    ins, outs, sems = refs[:count], refs[-1 - count : -1], refs[-1]
    copies = []
    for i, many in enumerate(pieces):
        step = ins[i].shape[1] // many
        for p in range(many):
            part = (slice(None), pl.ds(p * step, step))
            copies.append(pltpu.make_async_copy(ins[i].at[part], outs[i].at[part], sems.at[len(copies)]))
    for c in copies:
        c.start()
    for c in copies:
        c.wait()


def load(arrays, pieces, after=()):
    return pl.pallas_call(
        functools.partial(load_kernel, pieces),
        out_shape=[pltpu.VMEM(a.shape, a.dtype) for a in arrays],
        in_specs=[ANY] * (len(arrays) + len(after)),
        out_specs=[VM] * len(arrays),
        scratch_shapes=[pltpu.SemaphoreType.DMA((sum(pieces),))],
        compiler_params=pltpu.CompilerParams(vmem_limit_bytes=SMALL_LIMIT),
        cost_estimate=pl.CostEstimate(
            flops=0, bytes_accessed=2 * sum(a.size * a.dtype.itemsize for a in arrays), transcendentals=0
        ),
        name="load_weights",
    )(*[pltpu.with_memory_space_constraint(a, pltpu.HBM) for a in arrays], *after)


def attention(blocks, bias, js):
    rows, width = blocks[0].shape
    seen = jnp.concatenate([bias[j * rows : (j + 1) * rows] for j in js], axis=0)
    scores, values = [], []
    for h in range(width // (3 * DH)):
        c = h * 3 * DH
        q = jnp.concatenate([blocks[j][:, c : c + DH] for j in js], axis=0)
        k = jnp.concatenate([b[:, c + DH : c + 2 * DH] for b in blocks], axis=0)
        values.append(jnp.concatenate([b[:, c + 2 * DH : c + 3 * DH] for b in blocks], axis=0))
        scores.append(lax.dot_general(q, k, (((1,), (1,)), ((), ())), preferred_element_type=jnp.float32) + seen)
    tops = [jnp.max(s, axis=-1, keepdims=True) for s in scores]
    weights = [jnp.exp2((s - m) * (DH ** (-0.5) * math.log2(math.e))) for s, m in zip(scores, tops)]
    mixed = [
        jnp.dot(e.astype(jnp.bfloat16), jnp.concatenate([v, jnp.ones_like(v)], axis=1), preferred_element_type=jnp.float32)
        for e, v in zip(weights, values)
    ]
    attended = [(x[:, :DH] / x[:, DH:]).astype(jnp.bfloat16) for x in mixed]
    return jnp.concatenate(attended, axis=1)


def attend_project_kernel(n, js, *refs):
    blocks, bias, weight, near, far = refs[:n], refs[n], refs[n + 1], refs[n + 2], refs[n + 3]
    term = jnp.dot(attention(blocks, bias, js), weight[0], preferred_element_type=jnp.float32).astype(jnp.bfloat16)
    rows = near.shape[0]
    near[...] = term[:rows]
    far[...] = term[rows:]


def attend(blocks, bias, js, weight):
    n = len(blocks)
    rows, width = blocks[0].shape
    depth = weight.shape[2]
    queries = len(js) * rows
    return pl.pallas_call(
        functools.partial(attend_project_kernel, n, js),
        out_shape=[
            jax.ShapeDtypeStruct((rows, depth), jnp.bfloat16),
            jax.ShapeDtypeStruct((queries - rows, depth), jnp.bfloat16),
        ],
        in_specs=[VM] * (n + 2),
        out_specs=[VM, VM],
        compiler_params=pltpu.CompilerParams(vmem_limit_bytes=VMEM_LIMIT),
        cost_estimate=pl.CostEstimate(
            flops=2 * queries * width // 3 * (2 * n * rows + depth),
            bytes_accessed=2 * n * rows * width,
            transcendentals=queries * n * rows * width // (3 * DH),
        ),
        name="attend_project",
    )(*blocks, bias, weight)


def far_sum_kernel(rows, cols, mine, theirs, partial, *others):
    total = mine[...].astype(jnp.float32) + theirs[...].astype(jnp.float32)
    partial[...] = total[:, :cols].astype(jnp.bfloat16)
    for i, other in enumerate(others):
        other[...] = total[i * rows : (i + 1) * rows, cols:].astype(jnp.bfloat16)


def far_sum(mine, theirs, rows, cols):
    count, depth = mine.shape
    return pl.pallas_call(
        functools.partial(far_sum_kernel, rows, cols),
        out_shape=[jax.ShapeDtypeStruct((count, cols), jnp.bfloat16)]
        + [jax.ShapeDtypeStruct((rows, depth - cols), jnp.bfloat16)] * (count // rows),
        in_specs=[VM] * 2,
        out_specs=[VM] * (count // rows + 1),
        compiler_params=pltpu.CompilerParams(vmem_limit_bytes=VMEM_LIMIT),
        name="far_sum",
    )(mine, theirs)


def near_sum_kernel(mine, theirs, stream, far, partial, own):
    rows, cols = mine.shape[0], partial.shape[1]
    total = mine[...].astype(jnp.float32) + theirs[...].astype(jnp.float32) + stream[0].astype(jnp.float32)
    partial[:rows, :] = total[:, :cols].astype(jnp.bfloat16)
    partial[rows:, :] = far[...]
    own[...] = total[:, cols:]


def near_sum(mine, theirs, stream, far):
    rows, depth = mine.shape
    count, cols = far.shape
    return pl.pallas_call(
        near_sum_kernel,
        out_shape=[
            jax.ShapeDtypeStruct((rows + count, cols), jnp.bfloat16),
            jax.ShapeDtypeStruct((rows, depth - cols), jnp.float32),
        ],
        in_specs=[VM] * 4,
        out_specs=[VM] * 2,
        compiler_params=pltpu.CompilerParams(vmem_limit_bytes=SMALL_LIMIT),
        name="near_sum",
    )(mine, theirs, stream, far)


def settle_kernel(x, after, out):
    out[...] = x[...]


def settle(x, after):
    return pl.pallas_call(
        settle_kernel,
        out_shape=jax.ShapeDtypeStruct(x.shape, x.dtype),
        in_specs=[VM, ANY],
        out_specs=VM,
        compiler_params=pltpu.CompilerParams(vmem_limit_bytes=SMALL_LIMIT),
        name="settle",
    )(x, after)


def join_kernel(rows, mine, *refs):
    others, out = refs[:-1], refs[-1]
    for i in range(mine.shape[0] // rows):
        total = mine[i * rows : (i + 1) * rows, :].astype(jnp.float32)
        for k, other in enumerate(others):
            at = i ^ (k + 1)
            total = total + other[at * rows : (at + 1) * rows, :].astype(jnp.float32)
        out[i * rows : (i + 1) * rows, :] = total.astype(jnp.bfloat16)


def join(rows, mine, others):
    return pl.pallas_call(
        functools.partial(join_kernel, rows),
        out_shape=jax.ShapeDtypeStruct(mine.shape, mine.dtype),
        in_specs=[VM] * (1 + len(others)),
        out_specs=VM,
        compiler_params=pltpu.CompilerParams(vmem_limit_bytes=SMALL_LIMIT),
        name="join_chips",
    )(mine, *others)


def project_first_kernel(n, *refs):
    rest, gain, weight, total, squares, scaled = refs[:n], *refs[n:]
    rows, count = rest[0].shape
    cols = weight.shape[1] - count
    me = lax.axis_index("seq")
    for j in range(n):
        x = rest[j][...].astype(jnp.float32)
        here = pl.ds(pl.multiple_of((me ^ j) * rows, rows), rows)
        squares[here, :] = jnp.sum(x * x, axis=-1, keepdims=True)
        scaled[here, :] = (x * gain[:, cols:]).astype(jnp.bfloat16)
    total[...] = jnp.dot(scaled[...], weight[0, cols:, :], preferred_element_type=jnp.float32)


def project_first(rest, gain, weight):
    n = len(rest)
    rows, count = rest[0].shape
    width = weight.shape[2]
    tokens = n * rows
    return pl.pallas_call(
        functools.partial(project_first_kernel, n),
        out_shape=[
            jax.ShapeDtypeStruct((tokens, width), jnp.float32),
            jax.ShapeDtypeStruct((tokens, 1), jnp.float32),
        ],
        in_specs=[VM] * (n + 2),
        out_specs=[VM, VM],
        scratch_shapes=[pltpu.VMEM((tokens, count), jnp.bfloat16)],
        compiler_params=pltpu.CompilerParams(vmem_limit_bytes=VMEM_LIMIT),
        cost_estimate=pl.CostEstimate(
            flops=2 * tokens * count * width, bytes_accessed=2 * count * width, transcendentals=0
        ),
        name="project_first",
    )(*rest, gain, weight)


def project_second_kernel(n, tile, even, odd, rest, gain, weight, total, squares, kept, out, scaled, sums, made, sems):
    rows, cols = rest.shape[0], even.shape[1]
    depth, width = weight.shape[1:]
    me = lax.axis_index("seq")
    copies = [
        pltpu.make_async_copy(even.at[:rows], kept.at[0, :, pl.ds(0, cols)], sems.at[0]),
        pltpu.make_async_copy(rest, kept.at[0, :, pl.ds(cols, depth - cols)], sems.at[1]),
    ]
    for c in copies:
        c.start()
    for j in range(n):
        x = (odd if j % 2 else even)[j // 2 * rows : (j // 2 + 1) * rows, :].astype(jnp.float32)
        here = pl.ds(pl.multiple_of((me ^ j) * rows, rows), rows)
        sums[here, :] = squares[here, :] + jnp.sum(x * x, axis=-1, keepdims=True)
        scaled[here, :] = (x * gain[:, :cols]).astype(jnp.bfloat16)
    scale = lax.rsqrt(sums[...] / depth + 1e-06)
    for i in range(width // tile):
        part = pl.ds(i * tile, tile)
        mine = jnp.dot(scaled[...], weight[0, :cols, part], preferred_element_type=jnp.float32)
        made[:, part] = ((total[:, part] + mine) * scale).astype(jnp.bfloat16)
        copies.append(pltpu.make_async_copy(made.at[:, part], out.at[0, :, part], sems.at[2 + i]))
        copies[-1].start()
    for c in copies:
        c.wait()


def project_second(n, even, odd, rest, gain, weight, total, squares):
    rows = rest.shape[0]
    cols = even.shape[1]
    _, depth, width = weight.shape
    tile = 256 if width % 256 == 0 else 128
    return pl.pallas_call(
        functools.partial(project_second_kernel, n, tile),
        out_shape=[
            jax.ShapeDtypeStruct((1, rows, depth), jnp.bfloat16),
            jax.ShapeDtypeStruct((1, n * rows, width), jnp.bfloat16),
        ],
        in_specs=[VM] * 7,
        out_specs=[ANY, ANY],
        scratch_shapes=[
            pltpu.VMEM((n * rows, cols), jnp.bfloat16),
            pltpu.VMEM((n * rows, 1), jnp.float32),
            pltpu.VMEM((n * rows, width), jnp.bfloat16),
            pltpu.SemaphoreType.DMA((2 + width // tile,)),
        ],
        compiler_params=pltpu.CompilerParams(vmem_limit_bytes=VMEM_LIMIT),
        cost_estimate=pl.CostEstimate(
            flops=2 * n * rows * cols * width, bytes_accessed=2 * cols * width, transcendentals=0
        ),
        name="project_second",
    )(even, odd, rest, gain, weight, total, squares)


def mask_kernel(rows, mask, order, out):
    tokens = out.shape[0]
    windows, per, _ = mask.shape
    lanes = max(windows * per, 128)
    me = lax.axis_index("seq")
    row = lax.broadcasted_iota(jnp.int32, (tokens, tokens), 0)
    token = ((row // rows) ^ me) * rows + row % rows
    at = (order[...].reshape(1, tokens) == token).astype(jnp.bfloat16)
    position = lax.broadcasted_iota(jnp.int32, (tokens, lanes), 0)
    lane = lax.broadcasted_iota(jnp.int32, (tokens, lanes), 1)
    block = jnp.dot(
        at, (position // BLOCK == lane).astype(jnp.bfloat16), preferred_element_type=jnp.float32
    ).astype(jnp.bfloat16)
    first = lax.broadcasted_iota(jnp.int32, (lanes, lanes), 0)
    second = lax.broadcasted_iota(jnp.int32, (lanes, lanes), 1)
    visible = jnp.zeros((lanes, lanes), jnp.int32)
    for w in range(windows):
        for i in range(per):
            for j in range(per):
                here = (first == w * per + i) & (second == w * per + j)
                visible = jnp.where(here, mask[w, i, j], visible)
    visible = (visible > 0).astype(jnp.bfloat16)
    reach = jnp.dot(block, visible, preferred_element_type=jnp.float32).astype(jnp.bfloat16)
    seen = lax.dot_general(reach, block, (((1,), (1,)), ((), ())), preferred_element_type=jnp.float32)
    out[...] = jnp.where(seen > 0.5, 0.0, NEG)


def mask_bias(block_mask, token_order, n, rows):
    tokens = n * rows
    return pl.pallas_call(
        functools.partial(mask_kernel, rows),
        out_shape=jax.ShapeDtypeStruct((tokens, tokens), jnp.float32),
        in_specs=[pl.BlockSpec(memory_space=pltpu.SMEM), VM],
        out_specs=VM,
        compiler_params=pltpu.CompilerParams(vmem_limit_bytes=SMALL_LIMIT + 24 * tokens * tokens),
        name="mask_bias",
    )(block_mask, token_order)


def local(projected, stream_before, out_weight, proj_weight, norm_gain, block_mask, token_order):
    n = lax.axis_size("seq")
    rows = projected.shape[1]
    far_cut = cut(projected, n, tuple(range(2, n)))
    far = [swap(far_cut[j - 2], j) for j in range(2, n)]
    near_cut = cut(projected, n, (0, 1), (far_cut[-1],))
    blocks = [near_cut[0], swap(near_cut[1], 1)] + far
    stream, out_weight = load((stream_before, out_weight), (1, 4))
    bias = mask_bias(block_mask, token_order, n, rows)
    near_out, far_out = attend(blocks, bias, tuple(range(1, n, 2)), out_weight)
    near_own, far_own = attend(blocks, bias, tuple(range(0, n, 2)), out_weight)
    cols = out_weight.shape[2] * 7 // 16
    far_partial, *others = far_sum(far_own, swap(far_out, 1), rows, cols)
    partial, own = near_sum(near_own, swap(near_out, 1), stream, far_partial)
    partial = onward(partial, 0)
    (proj_weight,) = load((proj_weight,), (8,), (own,))
    total, proj_weight = lax.optimization_barrier((own, proj_weight))
    for k, x in enumerate(others):
        total = total + swap(x, 2 * k + 2).astype(jnp.float32)
    total = total.astype(jnp.bfloat16)
    rest = [onward(total, j) for j in range(0, n, 2)]
    partial = settle(partial, total)
    swapped = [swap(partial, j) for j in range(2, n, 2)]
    rest = [r for x in rest for r in (x, swap(x, 1))]
    swapped, rest = lax.optimization_barrier((swapped, rest))
    even = join(rows, partial, swapped)
    odd = swap(even, 1)
    total, squares = project_first(rest, norm_gain, proj_weight)
    kept, following = project_second(n, even, odd, rest[0], norm_gain, proj_weight, total, squares)
    return (kept, following)


def solution(mesh):
    placed = (
        P("segment", "seq", None),
        P("segment", "seq", None),
        P("segment", "seq", None),
        P("segment", None, "seq"),
        P("segment", None),
        P(),
        P(),
    )
    return jax.shard_map(
        local,
        mesh=mesh,
        in_specs=placed,
        out_specs=(P("segment", "seq", None), P("segment", None, "seq")),
        check_vma=False,
    )
```

```python
import functools
import math

import jax
import jax.numpy as jnp
from jax import lax
from jax.experimental import pallas as pl
from jax.experimental.pallas import tpu as pltpu
from jax.sharding import PartitionSpec as P

HEADS = 16
DH = 128
WIN = 256
BLOCK = 128
NEG = -1e30
VMEM_LIMIT = 16 * 1024 * 1024
SMALL_LIMIT = 4 * 1024 * 1024

VM = pl.BlockSpec(memory_space=pltpu.VMEM)
ANY = pl.BlockSpec(memory_space=pltpu.HBM)


def swap(x, by):
    size = lax.axis_size("seq")
    return lax.ppermute(x, "seq", [(i, i ^ by) for i in range(size)])


def onward(x, by):
    sections, size = lax.axis_size("segment"), lax.axis_size("seq")
    pairs = [
        (s * size + t, (s + 1) % sections * size + (t ^ by)) for s in range(sections) for t in range(size)
    ]
    return lax.ppermute(x, ("segment", "seq"), pairs)


def cut_kernel(js, src, *refs):
    outs, sems = refs[-1 - len(js) : -1], refs[-1]
    width = outs[0].shape[1]
    me = lax.axis_index("seq")
    copies = []
    for at, j in enumerate(js):
        first = pl.multiple_of((me ^ j) * width, 128)
        copies.append(pltpu.make_async_copy(src.at[0, :, pl.ds(first, width)], outs[at], sems.at[at]))
    for c in copies:
        c.start()
    for c in copies:
        c.wait()


def cut(projected, n, js, after=()):
    _, rows, columns = projected.shape
    width = columns // n
    return pl.pallas_call(
        functools.partial(cut_kernel, js),
        out_shape=[pltpu.VMEM((rows, width), projected.dtype)] * len(js),
        in_specs=[ANY] * (1 + len(after)),
        out_specs=[VM] * len(js),
        scratch_shapes=[pltpu.SemaphoreType.DMA((len(js),))],
        compiler_params=pltpu.CompilerParams(vmem_limit_bytes=SMALL_LIMIT),
        name="cut_slices",
    )(pltpu.with_memory_space_constraint(projected, pltpu.HBM), *after)


def load_kernel(pieces, *refs):
    count = len(pieces)
    ins, outs, sems = refs[:count], refs[-1 - count : -1], refs[-1]
    copies = []
    for i, many in enumerate(pieces):
        step = ins[i].shape[1] // many
        for p in range(many):
            part = (slice(None), pl.ds(p * step, step))
            copies.append(pltpu.make_async_copy(ins[i].at[part], outs[i].at[part], sems.at[len(copies)]))
    for c in copies:
        c.start()
    for c in copies:
        c.wait()


def load(arrays, pieces, after=()):
    return pl.pallas_call(
        functools.partial(load_kernel, pieces),
        out_shape=[pltpu.VMEM(a.shape, a.dtype) for a in arrays],
        in_specs=[ANY] * (len(arrays) + len(after)),
        out_specs=[VM] * len(arrays),
        scratch_shapes=[pltpu.SemaphoreType.DMA((sum(pieces),))],
        compiler_params=pltpu.CompilerParams(vmem_limit_bytes=SMALL_LIMIT),
        cost_estimate=pl.CostEstimate(
            flops=0, bytes_accessed=2 * sum(a.size * a.dtype.itemsize for a in arrays), transcendentals=0
        ),
        name="load_weights",
    )(*[pltpu.with_memory_space_constraint(a, pltpu.HBM) for a in arrays], *after)


def attention(blocks, bias, js):
    rows, width = blocks[0].shape
    seen = jnp.concatenate([bias[j * rows : (j + 1) * rows] for j in js], axis=0)
    scores, values = [], []
    for h in range(width // (3 * DH)):
        c = h * 3 * DH
        q = jnp.concatenate([blocks[j][:, c : c + DH] for j in js], axis=0)
        k = jnp.concatenate([b[:, c + DH : c + 2 * DH] for b in blocks], axis=0)
        values.append(jnp.concatenate([b[:, c + 2 * DH : c + 3 * DH] for b in blocks], axis=0))
        scores.append(lax.dot_general(q, k, (((1,), (1,)), ((), ())), preferred_element_type=jnp.float32) + seen)
    tops = [jnp.max(s, axis=-1, keepdims=True) for s in scores]
    weights = [jnp.exp2((s - m) * (DH ** (-0.5) * math.log2(math.e))) for s, m in zip(scores, tops)]
    mixed = [
        jnp.dot(e.astype(jnp.bfloat16), jnp.concatenate([v, jnp.ones_like(v)], axis=1), preferred_element_type=jnp.float32)
        for e, v in zip(weights, values)
    ]
    attended = [(x[:, :DH] / x[:, DH:]).astype(jnp.bfloat16) for x in mixed]
    return jnp.concatenate(attended, axis=1)


def attend_project_kernel(n, js, *refs):
    blocks, bias, weight, near, far = refs[:n], refs[n], refs[n + 1], refs[n + 2], refs[n + 3]
    term = jnp.dot(attention(blocks, bias, js), weight[0], preferred_element_type=jnp.float32).astype(jnp.bfloat16)
    rows = near.shape[0]
    near[...] = term[:rows]
    far[...] = term[rows:]


def attend(blocks, bias, js, weight):
    n = len(blocks)
    rows, width = blocks[0].shape
    depth = weight.shape[2]
    queries = len(js) * rows
    return pl.pallas_call(
        functools.partial(attend_project_kernel, n, js),
        out_shape=[
            jax.ShapeDtypeStruct((rows, depth), jnp.bfloat16),
            jax.ShapeDtypeStruct((queries - rows, depth), jnp.bfloat16),
        ],
        in_specs=[VM] * (n + 2),
        out_specs=[VM, VM],
        compiler_params=pltpu.CompilerParams(vmem_limit_bytes=VMEM_LIMIT),
        cost_estimate=pl.CostEstimate(
            flops=2 * queries * width // 3 * (2 * n * rows + depth),
            bytes_accessed=2 * n * rows * width,
            transcendentals=queries * n * rows * width // (3 * DH),
        ),
        name="attend_project",
    )(*blocks, bias, weight)


def far_sum_kernel(rows, cols, mine, theirs, partial, *others):
    total = mine[...].astype(jnp.float32) + theirs[...].astype(jnp.float32)
    partial[...] = total[:, :cols].astype(jnp.bfloat16)
    for i, other in enumerate(others):
        other[...] = total[i * rows : (i + 1) * rows, cols:].astype(jnp.bfloat16)


def far_sum(mine, theirs, rows, cols):
    count, depth = mine.shape
    return pl.pallas_call(
        functools.partial(far_sum_kernel, rows, cols),
        out_shape=[jax.ShapeDtypeStruct((count, cols), jnp.bfloat16)]
        + [jax.ShapeDtypeStruct((rows, depth - cols), jnp.bfloat16)] * (count // rows),
        in_specs=[VM] * 2,
        out_specs=[VM] * (count // rows + 1),
        compiler_params=pltpu.CompilerParams(vmem_limit_bytes=VMEM_LIMIT),
        name="far_sum",
    )(mine, theirs)


def near_sum_kernel(mine, theirs, stream, far, partial, own):
    rows, cols = mine.shape[0], partial.shape[1]
    total = mine[...].astype(jnp.float32) + theirs[...].astype(jnp.float32) + stream[0].astype(jnp.float32)
    partial[:rows, :] = total[:, :cols].astype(jnp.bfloat16)
    partial[rows:, :] = far[...]
    own[...] = total[:, cols:]


def near_sum(mine, theirs, stream, far):
    rows, depth = mine.shape
    count, cols = far.shape
    return pl.pallas_call(
        near_sum_kernel,
        out_shape=[
            jax.ShapeDtypeStruct((rows + count, cols), jnp.bfloat16),
            jax.ShapeDtypeStruct((rows, depth - cols), jnp.float32),
        ],
        in_specs=[VM] * 4,
        out_specs=[VM] * 2,
        compiler_params=pltpu.CompilerParams(vmem_limit_bytes=SMALL_LIMIT),
        name="near_sum",
    )(mine, theirs, stream, far)


def settle_kernel(x, after, out):
    out[...] = x[...]


def settle(x, after):
    return pl.pallas_call(
        settle_kernel,
        out_shape=jax.ShapeDtypeStruct(x.shape, x.dtype),
        in_specs=[VM, ANY],
        out_specs=VM,
        compiler_params=pltpu.CompilerParams(vmem_limit_bytes=SMALL_LIMIT),
        name="settle",
    )(x, after)


def join_kernel(rows, spare, mine, *refs):
    others, out = refs[: -1 - spare], refs[-1]
    for i in range(mine.shape[0] // rows):
        total = mine[i * rows : (i + 1) * rows, :].astype(jnp.float32)
        for k, other in enumerate(others):
            at = i ^ (k + 1)
            total = total + other[at * rows : (at + 1) * rows, :].astype(jnp.float32)
        out[i * rows : (i + 1) * rows, :] = total.astype(jnp.bfloat16)


def join(rows, mine, others, after):
    return pl.pallas_call(
        functools.partial(join_kernel, rows, len(after)),
        out_shape=jax.ShapeDtypeStruct(mine.shape, mine.dtype),
        in_specs=[VM] * (1 + len(others)) + [ANY] * len(after),
        out_specs=VM,
        compiler_params=pltpu.CompilerParams(vmem_limit_bytes=SMALL_LIMIT),
        name="join_chips",
    )(mine, *others, *after)


def project_rows_kernel(count, *refs):
    blocks, (gain, weight, total, squares, scaled) = refs[:count], refs[count:]
    rows, cols = blocks[0].shape
    here = slice(weight.shape[1] - cols, weight.shape[1])
    for i, block in enumerate(blocks):
        x = block[...].astype(jnp.float32)
        at = slice(i * rows, (i + 1) * rows)
        squares[at, :] = jnp.sum(x * x, axis=-1, keepdims=True)
        scaled[at, :] = (x * gain[:, here]).astype(jnp.bfloat16)
    total[...] = jnp.dot(scaled[...], weight[0, here, :], preferred_element_type=jnp.float32)


def project_rows(blocks, gain, weight):
    count = len(blocks)
    rows, cols = blocks[0].shape
    width = weight.shape[2]
    return pl.pallas_call(
        functools.partial(project_rows_kernel, count),
        out_shape=[
            jax.ShapeDtypeStruct((count * rows, width), jnp.float32),
            jax.ShapeDtypeStruct((count * rows, 1), jnp.float32),
        ],
        in_specs=[VM] * (count + 2),
        out_specs=[VM, VM],
        scratch_shapes=[pltpu.VMEM((count * rows, cols), jnp.bfloat16)],
        compiler_params=pltpu.CompilerParams(vmem_limit_bytes=VMEM_LIMIT),
        cost_estimate=pl.CostEstimate(
            flops=2 * count * rows * cols * width, bytes_accessed=2 * cols * width, transcendentals=0
        ),
        name="project_rows",
    )(*blocks, gain, weight)


def project_even_kernel(even, gain, weight, total, squares):
    cols = even.shape[1]
    x = even[...].astype(jnp.float32)
    squares[...] = jnp.sum(x * x, axis=-1, keepdims=True)
    scaled = (x * gain[:, :cols]).astype(jnp.bfloat16)
    total[...] = jnp.dot(scaled, weight[0, :cols, :], preferred_element_type=jnp.float32)


def project_even(even, gain, weight):
    count, cols = even.shape
    width = weight.shape[2]
    return pl.pallas_call(
        project_even_kernel,
        out_shape=[
            jax.ShapeDtypeStruct((count, width), jnp.float32),
            jax.ShapeDtypeStruct((count, 1), jnp.float32),
        ],
        in_specs=[VM] * 3,
        out_specs=[VM, VM],
        compiler_params=pltpu.CompilerParams(vmem_limit_bytes=VMEM_LIMIT),
        cost_estimate=pl.CostEstimate(
            flops=2 * count * cols * width, bytes_accessed=2 * cols * width, transcendentals=0
        ),
        name="project_even",
    )(even, gain, weight)


def project_odd_kernel(tile, odd, even, rest, gain, weight, *refs):
    near, near_squares, far, far_squares, even_total, even_squares, kept, out, made, sems = refs
    rows, cols = rest.shape[0], odd.shape[1]
    depth, width = weight.shape[1:]
    me = lax.axis_index("seq")
    copies = [
        pltpu.make_async_copy(even.at[:rows], kept.at[0, :, pl.ds(0, cols)], sems.at[0]),
        pltpu.make_async_copy(rest, kept.at[0, :, pl.ds(cols, depth - cols)], sems.at[1]),
    ]
    for c in copies:
        c.start()
    x = odd[...].astype(jnp.float32)
    odd_squares = jnp.sum(x * x, axis=-1, keepdims=True)
    scaled = (x * gain[:, :cols]).astype(jnp.bfloat16)
    places, scales = [], []
    for j in range(2 * odd.shape[0] // rows):
        at = pl.ds(pl.multiple_of((me ^ j) * rows, rows), rows)
        part = slice(j // 2 * rows, (j // 2 + 1) * rows)
        total, squares = (near, near_squares) if j < 2 else (far, far_squares)
        here = slice(j % 2 * rows, (j % 2 + 1) * rows) if j < 2 else slice((j - 2) * rows, (j - 1) * rows)
        mine = odd_squares[part] if j % 2 else even_squares[part, :]
        places.append((at, part, total, here))
        scales.append(lax.rsqrt((squares[here, :] + mine) / depth + 1e-06))
    for i in range(width // tile):
        lanes = pl.ds(i * tile, tile)
        product = jnp.dot(scaled, weight[0, :cols, lanes], preferred_element_type=jnp.float32)
        for j, (at, part, total, here) in enumerate(places):
            mine = product[part] if j % 2 else even_total[part, lanes]
            made[at, lanes] = ((total[here, lanes] + mine) * scales[j]).astype(jnp.bfloat16)
        copies.append(pltpu.make_async_copy(made.at[:, lanes], out.at[0, :, lanes], sems.at[2 + i]))
        copies[-1].start()
    for c in copies:
        c.wait()


def project_odd(n, odd, even, rest, gain, weight, near, far, evens):
    rows = rest.shape[0]
    _, depth, width = weight.shape
    tile = 256 if width % 256 == 0 else 128
    return pl.pallas_call(
        functools.partial(project_odd_kernel, tile),
        out_shape=[
            jax.ShapeDtypeStruct((1, rows, depth), jnp.bfloat16),
            jax.ShapeDtypeStruct((1, n * rows, width), jnp.bfloat16),
        ],
        in_specs=[VM] * 11,
        out_specs=[ANY, ANY],
        scratch_shapes=[
            pltpu.VMEM((n * rows, width), jnp.bfloat16),
            pltpu.SemaphoreType.DMA((2 + width // tile,)),
        ],
        compiler_params=pltpu.CompilerParams(vmem_limit_bytes=VMEM_LIMIT),
        cost_estimate=pl.CostEstimate(
            flops=n * rows * odd.shape[1] * width, bytes_accessed=2 * odd.shape[1] * width, transcendentals=0
        ),
        name="project_odd",
    )(odd, even, rest, gain, weight, *near, *far, *evens)


def mask_kernel(rows, mask, order, out):
    tokens = out.shape[0]
    windows, per, _ = mask.shape
    lanes = max(windows * per, 128)
    me = lax.axis_index("seq")
    row = lax.broadcasted_iota(jnp.int32, (tokens, tokens), 0)
    token = ((row // rows) ^ me) * rows + row % rows
    at = (order[...].reshape(1, tokens) == token).astype(jnp.bfloat16)
    position = lax.broadcasted_iota(jnp.int32, (tokens, lanes), 0)
    lane = lax.broadcasted_iota(jnp.int32, (tokens, lanes), 1)
    block = jnp.dot(
        at, (position // BLOCK == lane).astype(jnp.bfloat16), preferred_element_type=jnp.float32
    ).astype(jnp.bfloat16)
    first = lax.broadcasted_iota(jnp.int32, (lanes, lanes), 0)
    second = lax.broadcasted_iota(jnp.int32, (lanes, lanes), 1)
    visible = jnp.zeros((lanes, lanes), jnp.int32)
    for w in range(windows):
        for i in range(per):
            for j in range(per):
                here = (first == w * per + i) & (second == w * per + j)
                visible = jnp.where(here, mask[w, i, j], visible)
    visible = (visible > 0).astype(jnp.bfloat16)
    reach = jnp.dot(block, visible, preferred_element_type=jnp.float32).astype(jnp.bfloat16)
    seen = lax.dot_general(reach, block, (((1,), (1,)), ((), ())), preferred_element_type=jnp.float32)
    out[...] = jnp.where(seen > 0.5, 0.0, NEG)


def mask_bias(block_mask, token_order, n, rows):
    tokens = n * rows
    return pl.pallas_call(
        functools.partial(mask_kernel, rows),
        out_shape=jax.ShapeDtypeStruct((tokens, tokens), jnp.float32),
        in_specs=[pl.BlockSpec(memory_space=pltpu.SMEM), VM],
        out_specs=VM,
        compiler_params=pltpu.CompilerParams(vmem_limit_bytes=SMALL_LIMIT + 24 * tokens * tokens),
        name="mask_bias",
    )(block_mask, token_order)


def local(projected, stream_before, out_weight, proj_weight, norm_gain, block_mask, token_order):
    n = lax.axis_size("seq")
    rows = projected.shape[1]
    far_cut = cut(projected, n, tuple(range(2, n)))
    far = [swap(far_cut[j - 2], j) for j in range(2, n)]
    near_cut = cut(projected, n, (0, 1), (far_cut[-1],))
    blocks = [near_cut[0], swap(near_cut[1], 1)] + far
    stream, out_weight = load((stream_before, out_weight), (1, 4))
    bias = mask_bias(block_mask, token_order, n, rows)
    near_out, far_out = attend(blocks, bias, tuple(range(1, n, 2)), out_weight)
    near_own, far_own = attend(blocks, bias, tuple(range(0, n, 2)), out_weight)
    cols = out_weight.shape[2] * 7 // 16
    far_partial, *others = far_sum(far_own, swap(far_out, 1), rows, cols)
    partial, own = near_sum(near_own, swap(near_out, 1), stream, far_partial)
    partial = onward(partial, 0)
    (proj_weight,) = load((proj_weight,), (8,), (own,))
    total, proj_weight = lax.optimization_barrier((own, proj_weight))
    for k, x in enumerate(others):
        total = total + swap(x, 2 * k + 2).astype(jnp.float32)
    total = total.astype(jnp.bfloat16)
    rest = [onward(total, j) for j in range(0, n, 2)]
    partial = settle(partial, total)
    swapped = [swap(partial, j) for j in range(2, n, 2)]
    rest = [r for x in rest for r in (x, swap(x, 1))]
    far_total = project_rows(rest[2:], norm_gain, proj_weight)
    even = join(rows, partial, swapped, (*far_total, *rest[:2]))
    odd = swap(even, 1)
    near_total = project_rows(rest[:2], norm_gain, proj_weight)
    even_total = project_even(even, norm_gain, proj_weight)
    return project_odd(n, odd, even, rest[0], norm_gain, proj_weight, near_total, far_total, even_total)


def solution(mesh):
    placed = (
        P("segment", "seq", None),
        P("segment", "seq", None),
        P("segment", "seq", None),
        P("segment", None, "seq"),
        P("segment", None),
        P(),
        P(),
    )
    return jax.shard_map(
        local,
        mesh=mesh,
        in_specs=placed,
        out_specs=(P("segment", "seq", None), P("segment", None, "seq")),
        check_vma=False,
    )
```

```python
import functools
import math

import jax
import jax.numpy as jnp
from jax import lax
from jax.experimental import pallas as pl
from jax.experimental.pallas import tpu as pltpu
from jax.sharding import PartitionSpec as P

HEADS = 16
DH = 128
WIN = 256
BLOCK = 128
NEG = -1e30
VMEM_LIMIT = 16 * 1024 * 1024
SMALL_LIMIT = 4 * 1024 * 1024

VM = pl.BlockSpec(memory_space=pltpu.VMEM)
ANY = pl.BlockSpec(memory_space=pltpu.HBM)


def swap(x, by):
    size = lax.axis_size("seq")
    return lax.ppermute(x, "seq", [(i, i ^ by) for i in range(size)])


def onward(x, by):
    sections, size = lax.axis_size("segment"), lax.axis_size("seq")
    pairs = [
        (s * size + t, (s + 1) % sections * size + (t ^ by)) for s in range(sections) for t in range(size)
    ]
    return lax.ppermute(x, ("segment", "seq"), pairs)


def cut_kernel(js, src, *refs):
    outs, sems = refs[-1 - len(js) : -1], refs[-1]
    width = outs[0].shape[1]
    me = lax.axis_index("seq")
    copies = []
    for at, j in enumerate(js):
        first = pl.multiple_of((me ^ j) * width, 128)
        copies.append(pltpu.make_async_copy(src.at[0, :, pl.ds(first, width)], outs[at], sems.at[at]))
    for c in copies:
        c.start()
    for c in copies:
        c.wait()


def cut(projected, n, js, after=()):
    _, rows, columns = projected.shape
    width = columns // n
    return pl.pallas_call(
        functools.partial(cut_kernel, js),
        out_shape=[pltpu.VMEM((rows, width), projected.dtype)] * len(js),
        in_specs=[ANY] * (1 + len(after)),
        out_specs=[VM] * len(js),
        scratch_shapes=[pltpu.SemaphoreType.DMA((len(js),))],
        compiler_params=pltpu.CompilerParams(vmem_limit_bytes=SMALL_LIMIT),
        name="cut_slices",
    )(pltpu.with_memory_space_constraint(projected, pltpu.HBM), *after)


def load_kernel(pieces, *refs):
    count = len(pieces)
    ins, outs, sems = refs[:count], refs[-1 - count : -1], refs[-1]
    copies = []
    for i, many in enumerate(pieces):
        step = ins[i].shape[1] // many
        for p in range(many):
            part = (slice(None), pl.ds(p * step, step))
            copies.append(pltpu.make_async_copy(ins[i].at[part], outs[i].at[part], sems.at[len(copies)]))
    for c in copies:
        c.start()
    for c in copies:
        c.wait()


def load(arrays, pieces, after=()):
    return pl.pallas_call(
        functools.partial(load_kernel, pieces),
        out_shape=[pltpu.VMEM(a.shape, a.dtype) for a in arrays],
        in_specs=[ANY] * (len(arrays) + len(after)),
        out_specs=[VM] * len(arrays),
        scratch_shapes=[pltpu.SemaphoreType.DMA((sum(pieces),))],
        compiler_params=pltpu.CompilerParams(vmem_limit_bytes=SMALL_LIMIT),
        cost_estimate=pl.CostEstimate(
            flops=0, bytes_accessed=2 * sum(a.size * a.dtype.itemsize for a in arrays), transcendentals=0
        ),
        name="load_weights",
    )(*[pltpu.with_memory_space_constraint(a, pltpu.HBM) for a in arrays], *after)


def attention(blocks, bias, js):
    rows, width = blocks[0].shape
    seen = jnp.concatenate([bias[j * rows : (j + 1) * rows] for j in js], axis=0)
    scores, values = [], []
    for h in range(width // (3 * DH)):
        c = h * 3 * DH
        q = jnp.concatenate([blocks[j][:, c : c + DH] for j in js], axis=0)
        k = jnp.concatenate([b[:, c + DH : c + 2 * DH] for b in blocks], axis=0)
        values.append(jnp.concatenate([b[:, c + 2 * DH : c + 3 * DH] for b in blocks], axis=0))
        scores.append(lax.dot_general(q, k, (((1,), (1,)), ((), ())), preferred_element_type=jnp.float32) + seen)
    tops = [jnp.max(s, axis=-1, keepdims=True) for s in scores]
    weights = [jnp.exp2((s - m) * (DH ** (-0.5) * math.log2(math.e))) for s, m in zip(scores, tops)]
    mixed = [
        jnp.dot(e.astype(jnp.bfloat16), jnp.concatenate([v, jnp.ones_like(v)], axis=1), preferred_element_type=jnp.float32)
        for e, v in zip(weights, values)
    ]
    attended = [(x[:, :DH] / x[:, DH:]).astype(jnp.bfloat16) for x in mixed]
    return jnp.concatenate(attended, axis=1)


def attend_project_kernel(n, js, *refs):
    blocks, bias, weight, near, far = refs[:n], refs[n], refs[n + 1], refs[n + 2], refs[n + 3]
    attended = attention(blocks, bias, js)
    rows, depth = near.shape
    for i in range(4):
        part = slice(i * depth // 4, (i + 1) * depth // 4)
        term = jnp.dot(attended, weight[0, :, part], preferred_element_type=jnp.float32).astype(jnp.bfloat16)
        near[:, part] = term[:rows]
        far[:, part] = term[rows:]


def attend(blocks, bias, js, weight):
    n = len(blocks)
    rows, width = blocks[0].shape
    depth = weight.shape[2]
    queries = len(js) * rows
    return pl.pallas_call(
        functools.partial(attend_project_kernel, n, js),
        out_shape=[
            jax.ShapeDtypeStruct((rows, depth), jnp.bfloat16),
            jax.ShapeDtypeStruct((queries - rows, depth), jnp.bfloat16),
        ],
        in_specs=[VM] * (n + 2),
        out_specs=[VM, VM],
        compiler_params=pltpu.CompilerParams(vmem_limit_bytes=VMEM_LIMIT),
        cost_estimate=pl.CostEstimate(
            flops=2 * queries * width // 3 * (2 * n * rows + depth),
            bytes_accessed=2 * n * rows * width,
            transcendentals=queries * n * rows * width // (3 * DH),
        ),
        name="attend_project",
    )(*blocks, bias, weight)


def far_sum_kernel(rows, cols, mine, theirs, partial, *others):
    total = mine[...].astype(jnp.float32) + theirs[...].astype(jnp.float32)
    partial[...] = total[:, :cols].astype(jnp.bfloat16)
    for i, other in enumerate(others):
        other[...] = total[i * rows : (i + 1) * rows, cols:].astype(jnp.bfloat16)


def far_sum(mine, theirs, rows, cols):
    count, depth = mine.shape
    return pl.pallas_call(
        functools.partial(far_sum_kernel, rows, cols),
        out_shape=[jax.ShapeDtypeStruct((count, cols), jnp.bfloat16)]
        + [jax.ShapeDtypeStruct((rows, depth - cols), jnp.bfloat16)] * (count // rows),
        in_specs=[VM] * 2,
        out_specs=[VM] * (count // rows + 1),
        compiler_params=pltpu.CompilerParams(vmem_limit_bytes=VMEM_LIMIT),
        name="far_sum",
    )(mine, theirs)


def near_sum_kernel(mine, theirs, stream, far, partial, own):
    rows, cols = mine.shape[0], partial.shape[1]
    total = mine[...].astype(jnp.float32) + theirs[...].astype(jnp.float32) + stream[0].astype(jnp.float32)
    partial[:rows, :] = total[:, :cols].astype(jnp.bfloat16)
    partial[rows:, :] = far[...]
    own[...] = total[:, cols:]


def near_sum(mine, theirs, stream, far):
    rows, depth = mine.shape
    count, cols = far.shape
    return pl.pallas_call(
        near_sum_kernel,
        out_shape=[
            jax.ShapeDtypeStruct((rows + count, cols), jnp.bfloat16),
            jax.ShapeDtypeStruct((rows, depth - cols), jnp.float32),
        ],
        in_specs=[VM] * 4,
        out_specs=[VM] * 2,
        compiler_params=pltpu.CompilerParams(vmem_limit_bytes=SMALL_LIMIT),
        name="near_sum",
    )(mine, theirs, stream, far)


def settle_kernel(x, after, out):
    out[...] = x[...]


def settle(x, after):
    return pl.pallas_call(
        settle_kernel,
        out_shape=jax.ShapeDtypeStruct(x.shape, x.dtype),
        in_specs=[VM, ANY],
        out_specs=VM,
        compiler_params=pltpu.CompilerParams(vmem_limit_bytes=SMALL_LIMIT),
        name="settle",
    )(x, after)


def join_kernel(rows, spare, mine, *refs):
    others, out = refs[: -1 - spare], refs[-1]
    for i in range(mine.shape[0] // rows):
        total = mine[i * rows : (i + 1) * rows, :].astype(jnp.float32)
        for k, other in enumerate(others):
            at = i ^ (k + 1)
            total = total + other[at * rows : (at + 1) * rows, :].astype(jnp.float32)
        out[i * rows : (i + 1) * rows, :] = total.astype(jnp.bfloat16)


def join(rows, mine, others, after):
    return pl.pallas_call(
        functools.partial(join_kernel, rows, len(after)),
        out_shape=jax.ShapeDtypeStruct(mine.shape, mine.dtype),
        in_specs=[VM] * (1 + len(others)) + [ANY] * len(after),
        out_specs=VM,
        compiler_params=pltpu.CompilerParams(vmem_limit_bytes=SMALL_LIMIT),
        name="join_chips",
    )(mine, *others, *after)


def project_rows_kernel(count, *refs):
    blocks, (gain, weight, total, squares, scaled) = refs[:count], refs[count:]
    rows, cols = blocks[0].shape
    here = slice(weight.shape[1] - cols, weight.shape[1])
    for i, block in enumerate(blocks):
        x = block[...].astype(jnp.float32)
        at = slice(i * rows, (i + 1) * rows)
        squares[at, :] = jnp.sum(x * x, axis=-1, keepdims=True)
        scaled[at, :] = (x * gain[:, here]).astype(jnp.bfloat16)
    total[...] = jnp.dot(scaled[...], weight[0, here, :], preferred_element_type=jnp.float32)


def project_rows(blocks, gain, weight):
    count = len(blocks)
    rows, cols = blocks[0].shape
    width = weight.shape[2]
    return pl.pallas_call(
        functools.partial(project_rows_kernel, count),
        out_shape=[
            jax.ShapeDtypeStruct((count * rows, width), jnp.float32),
            jax.ShapeDtypeStruct((count * rows, 1), jnp.float32),
        ],
        in_specs=[VM] * (count + 2),
        out_specs=[VM, VM],
        scratch_shapes=[pltpu.VMEM((count * rows, cols), jnp.bfloat16)],
        compiler_params=pltpu.CompilerParams(vmem_limit_bytes=VMEM_LIMIT),
        cost_estimate=pl.CostEstimate(
            flops=2 * count * rows * cols * width, bytes_accessed=2 * cols * width, transcendentals=0
        ),
        name="project_rows",
    )(*blocks, gain, weight)


def project_even_kernel(even, gain, weight, total, squares):
    cols = even.shape[1]
    x = even[...].astype(jnp.float32)
    squares[...] = jnp.sum(x * x, axis=-1, keepdims=True)
    scaled = (x * gain[:, :cols]).astype(jnp.bfloat16)
    total[...] = jnp.dot(scaled, weight[0, :cols, :], preferred_element_type=jnp.float32)


def project_even(even, gain, weight):
    count, cols = even.shape
    width = weight.shape[2]
    return pl.pallas_call(
        project_even_kernel,
        out_shape=[
            jax.ShapeDtypeStruct((count, width), jnp.float32),
            jax.ShapeDtypeStruct((count, 1), jnp.float32),
        ],
        in_specs=[VM] * 3,
        out_specs=[VM, VM],
        compiler_params=pltpu.CompilerParams(vmem_limit_bytes=VMEM_LIMIT),
        cost_estimate=pl.CostEstimate(
            flops=2 * count * cols * width, bytes_accessed=2 * cols * width, transcendentals=0
        ),
        name="project_even",
    )(even, gain, weight)


def project_odd_kernel(tile, odd, even, rest, gain, weight, *refs):
    near, near_squares, far, far_squares, even_total, even_squares, kept, out, made, sems = refs
    rows, cols = rest.shape[0], odd.shape[1]
    depth, width = weight.shape[1:]
    me = lax.axis_index("seq")
    copies = [
        pltpu.make_async_copy(even.at[:rows], kept.at[0, :, pl.ds(0, cols)], sems.at[0]),
        pltpu.make_async_copy(rest, kept.at[0, :, pl.ds(cols, depth - cols)], sems.at[1]),
    ]
    for c in copies:
        c.start()
    x = odd[...].astype(jnp.float32)
    odd_squares = jnp.sum(x * x, axis=-1, keepdims=True)
    scaled = (x * gain[:, :cols]).astype(jnp.bfloat16)
    places, scales = [], []
    for j in range(2 * odd.shape[0] // rows):
        at = pl.ds(pl.multiple_of((me ^ j) * rows, rows), rows)
        part = slice(j // 2 * rows, (j // 2 + 1) * rows)
        total, squares = (near, near_squares) if j < 2 else (far, far_squares)
        here = slice(j % 2 * rows, (j % 2 + 1) * rows) if j < 2 else slice((j - 2) * rows, (j - 1) * rows)
        mine = odd_squares[part] if j % 2 else even_squares[part, :]
        places.append((at, part, total, here))
        scales.append(lax.rsqrt((squares[here, :] + mine) / depth + 1e-06))
    for i in range(width // tile):
        lanes = pl.ds(i * tile, tile)
        product = jnp.dot(scaled, weight[0, :cols, lanes], preferred_element_type=jnp.float32)
        for j, (at, part, total, here) in enumerate(places):
            mine = product[part] if j % 2 else even_total[part, lanes]
            made[at, lanes] = ((total[here, lanes] + mine) * scales[j]).astype(jnp.bfloat16)
        copies.append(pltpu.make_async_copy(made.at[:, lanes], out.at[0, :, lanes], sems.at[2 + i]))
        copies[-1].start()
    for c in copies:
        c.wait()


def project_odd(n, odd, even, rest, gain, weight, near, far, evens):
    rows = rest.shape[0]
    _, depth, width = weight.shape
    tile = 256 if width % 256 == 0 else 128
    return pl.pallas_call(
        functools.partial(project_odd_kernel, tile),
        out_shape=[
            jax.ShapeDtypeStruct((1, rows, depth), jnp.bfloat16),
            jax.ShapeDtypeStruct((1, n * rows, width), jnp.bfloat16),
        ],
        in_specs=[VM] * 11,
        out_specs=[ANY, ANY],
        scratch_shapes=[
            pltpu.VMEM((n * rows, width), jnp.bfloat16),
            pltpu.SemaphoreType.DMA((2 + width // tile,)),
        ],
        compiler_params=pltpu.CompilerParams(vmem_limit_bytes=VMEM_LIMIT),
        cost_estimate=pl.CostEstimate(
            flops=n * rows * odd.shape[1] * width, bytes_accessed=2 * odd.shape[1] * width, transcendentals=0
        ),
        name="project_odd",
    )(odd, even, rest, gain, weight, *near, *far, *evens)


def mask_kernel(rows, mask, order, out):
    tokens = out.shape[0]
    windows, per, _ = mask.shape
    lanes = max(windows * per, 128)
    me = lax.axis_index("seq")
    row = lax.broadcasted_iota(jnp.int32, (tokens, tokens), 0)
    token = ((row // rows) ^ me) * rows + row % rows
    at = (order[...].reshape(1, tokens) == token).astype(jnp.bfloat16)
    position = lax.broadcasted_iota(jnp.int32, (tokens, lanes), 0)
    lane = lax.broadcasted_iota(jnp.int32, (tokens, lanes), 1)
    block = jnp.dot(
        at, (position // BLOCK == lane).astype(jnp.bfloat16), preferred_element_type=jnp.float32
    ).astype(jnp.bfloat16)
    first = lax.broadcasted_iota(jnp.int32, (lanes, lanes), 0)
    second = lax.broadcasted_iota(jnp.int32, (lanes, lanes), 1)
    visible = jnp.zeros((lanes, lanes), jnp.int32)
    for w in range(windows):
        for i in range(per):
            for j in range(per):
                here = (first == w * per + i) & (second == w * per + j)
                visible = jnp.where(here, mask[w, i, j], visible)
    visible = (visible > 0).astype(jnp.bfloat16)
    reach = jnp.dot(block, visible, preferred_element_type=jnp.float32).astype(jnp.bfloat16)
    seen = lax.dot_general(reach, block, (((1,), (1,)), ((), ())), preferred_element_type=jnp.float32)
    out[...] = jnp.where(seen > 0.5, 0.0, NEG)


def mask_bias(block_mask, token_order, n, rows):
    tokens = n * rows
    return pl.pallas_call(
        functools.partial(mask_kernel, rows),
        out_shape=jax.ShapeDtypeStruct((tokens, tokens), jnp.float32),
        in_specs=[pl.BlockSpec(memory_space=pltpu.SMEM), VM],
        out_specs=VM,
        compiler_params=pltpu.CompilerParams(vmem_limit_bytes=SMALL_LIMIT + 24 * tokens * tokens),
        name="mask_bias",
    )(block_mask, token_order)


def local(projected, stream_before, out_weight, proj_weight, norm_gain, block_mask, token_order):
    n = lax.axis_size("seq")
    rows = projected.shape[1]
    far_cut = cut(projected, n, tuple(range(2, n)))
    far = [swap(far_cut[j - 2], j) for j in range(2, n)]
    near_cut = cut(projected, n, (0, 1), (far_cut[-1],))
    blocks = [near_cut[0], swap(near_cut[1], 1)] + far
    stream, out_weight = load((stream_before, out_weight), (1, 4))
    bias = mask_bias(block_mask, token_order, n, rows)
    near_out, far_out = attend(blocks, bias, tuple(range(1, n, 2)), out_weight)
    near_own, far_own = attend(blocks, bias, tuple(range(0, n, 2)), out_weight)
    cols = out_weight.shape[2] * 7 // 16
    far_partial, *others = far_sum(far_own, swap(far_out, 1), rows, cols)
    partial, own = near_sum(near_own, swap(near_out, 1), stream, far_partial)
    partial = onward(partial, 0)
    (proj_weight,) = load((proj_weight,), (8,), (own,))
    total, proj_weight = lax.optimization_barrier((own, proj_weight))
    for k, x in enumerate(others):
        total = total + swap(x, 2 * k + 2).astype(jnp.float32)
    total = total.astype(jnp.bfloat16)
    rest = [onward(total, j) for j in range(0, n, 2)]
    partial = settle(partial, total)
    swapped = [swap(partial, j) for j in range(2, n, 2)]
    rest = [r for x in rest for r in (x, swap(x, 1))]
    far_total = project_rows(rest[2:], norm_gain, proj_weight)
    even = join(rows, partial, swapped, (*far_total, *rest[:2]))
    odd = swap(even, 1)
    near_total = project_rows(rest[:2], norm_gain, proj_weight)
    even_total = project_even(even, norm_gain, proj_weight)
    return project_odd(n, odd, even, rest[0], norm_gain, proj_weight, near_total, far_total, even_total)


def solution(mesh):
    placed = (
        P("segment", "seq", None),
        P("segment", "seq", None),
        P("segment", "seq", None),
        P("segment", None, "seq"),
        P("segment", None),
        P(),
        P(),
    )
    return jax.shard_map(
        local,
        mesh=mesh,
        in_specs=placed,
        out_specs=(P("segment", "seq", None), P("segment", None, "seq")),
        check_vma=False,
    )
```

```python
import functools
import math

import jax
import jax.numpy as jnp
from jax import lax
from jax.experimental import pallas as pl
from jax.experimental.pallas import tpu as pltpu
from jax.sharding import PartitionSpec as P

HEADS = 16
DH = 128
WIN = 256
BLOCK = 128
NEG = -1e30
VMEM_LIMIT = 16 * 1024 * 1024
SMALL_LIMIT = 4 * 1024 * 1024

VM = pl.BlockSpec(memory_space=pltpu.VMEM)
ANY = pl.BlockSpec(memory_space=pltpu.HBM)


def swap(x, by):
    size = lax.axis_size("seq")
    return lax.ppermute(x, "seq", [(i, i ^ by) for i in range(size)])


def onward(x, by):
    sections, size = lax.axis_size("segment"), lax.axis_size("seq")
    pairs = [
        (s * size + t, (s + 1) % sections * size + (t ^ by)) for s in range(sections) for t in range(size)
    ]
    return lax.ppermute(x, ("segment", "seq"), pairs)


def cut_kernel(js, src, *refs):
    outs, sems = refs[-1 - len(js) : -1], refs[-1]
    width = outs[0].shape[1]
    me = lax.axis_index("seq")
    copies = []
    for at, j in enumerate(js):
        first = pl.multiple_of((me ^ j) * width, 128)
        copies.append(pltpu.make_async_copy(src.at[0, :, pl.ds(first, width)], outs[at], sems.at[at]))
    for c in copies:
        c.start()
    for c in copies:
        c.wait()


def cut(projected, n, js, after=()):
    _, rows, columns = projected.shape
    width = columns // n
    return pl.pallas_call(
        functools.partial(cut_kernel, js),
        out_shape=[pltpu.VMEM((rows, width), projected.dtype)] * len(js),
        in_specs=[ANY] * (1 + len(after)),
        out_specs=[VM] * len(js),
        scratch_shapes=[pltpu.SemaphoreType.DMA((len(js),))],
        compiler_params=pltpu.CompilerParams(vmem_limit_bytes=SMALL_LIMIT),
        name="cut_slices",
    )(pltpu.with_memory_space_constraint(projected, pltpu.HBM), *after)


def load_kernel(pieces, *refs):
    count = len(pieces)
    ins, outs, sems = refs[:count], refs[-1 - count : -1], refs[-1]
    copies = []
    for i, many in enumerate(pieces):
        step = ins[i].shape[1] // many
        for p in range(many):
            part = (slice(None), pl.ds(p * step, step))
            copies.append(pltpu.make_async_copy(ins[i].at[part], outs[i].at[part], sems.at[len(copies)]))
    for c in copies:
        c.start()
    for c in copies:
        c.wait()


def load(arrays, pieces, after=()):
    return pl.pallas_call(
        functools.partial(load_kernel, pieces),
        out_shape=[pltpu.VMEM(a.shape, a.dtype) for a in arrays],
        in_specs=[ANY] * (len(arrays) + len(after)),
        out_specs=[VM] * len(arrays),
        scratch_shapes=[pltpu.SemaphoreType.DMA((sum(pieces),))],
        compiler_params=pltpu.CompilerParams(vmem_limit_bytes=SMALL_LIMIT),
        cost_estimate=pl.CostEstimate(
            flops=0, bytes_accessed=2 * sum(a.size * a.dtype.itemsize for a in arrays), transcendentals=0
        ),
        name="load_weights",
    )(*[pltpu.with_memory_space_constraint(a, pltpu.HBM) for a in arrays], *after)


def attention(blocks, bias, js):
    rows, width = blocks[0].shape
    seen = jnp.concatenate([bias[j * rows : (j + 1) * rows] for j in js], axis=0)
    scores, values = [], []
    for h in range(width // (3 * DH)):
        c = h * 3 * DH
        q = jnp.concatenate([blocks[j][:, c : c + DH] for j in js], axis=0)
        k = jnp.concatenate([b[:, c + DH : c + 2 * DH] for b in blocks], axis=0)
        values.append(jnp.concatenate([b[:, c + 2 * DH : c + 3 * DH] for b in blocks], axis=0))
        scores.append(lax.dot_general(q, k, (((1,), (1,)), ((), ())), preferred_element_type=jnp.float32) + seen)
    tops = [jnp.max(s, axis=-1, keepdims=True) for s in scores]
    weights = [jnp.exp2((s - m) * (DH ** (-0.5) * math.log2(math.e))) for s, m in zip(scores, tops)]
    mixed = [
        jnp.dot(e.astype(jnp.bfloat16), jnp.concatenate([v, jnp.ones_like(v)], axis=1), preferred_element_type=jnp.float32)
        for e, v in zip(weights, values)
    ]
    attended = [(x[:, :DH] / x[:, DH:]).astype(jnp.bfloat16) for x in mixed]
    return jnp.concatenate(attended, axis=1)


def attend_project_kernel(n, js, *refs):
    blocks, bias, weight, near, far = refs[:n], refs[n], refs[n + 1], refs[n + 2], refs[n + 3]
    term = jnp.dot(attention(blocks, bias, js), weight[0], preferred_element_type=jnp.float32).astype(jnp.bfloat16)
    rows = near.shape[0]
    near[...] = term[:rows]
    far[...] = term[rows:]


def attend(blocks, bias, js, weight):
    n = len(blocks)
    rows, width = blocks[0].shape
    depth = weight.shape[2]
    queries = len(js) * rows
    return pl.pallas_call(
        functools.partial(attend_project_kernel, n, js),
        out_shape=[
            jax.ShapeDtypeStruct((rows, depth), jnp.bfloat16),
            jax.ShapeDtypeStruct((queries - rows, depth), jnp.bfloat16),
        ],
        in_specs=[VM] * (n + 2),
        out_specs=[VM, VM],
        compiler_params=pltpu.CompilerParams(vmem_limit_bytes=VMEM_LIMIT),
        cost_estimate=pl.CostEstimate(
            flops=2 * queries * width // 3 * (2 * n * rows + depth),
            bytes_accessed=2 * n * rows * width,
            transcendentals=queries * n * rows * width // (3 * DH),
        ),
        name="attend_project",
    )(*blocks, bias, weight)


def far_sum_kernel(rows, cols, mine, theirs, partial, *others):
    total = mine[...].astype(jnp.float32) + theirs[...].astype(jnp.float32)
    partial[...] = total[:, :cols].astype(jnp.bfloat16)
    for i, other in enumerate(others):
        other[...] = total[i * rows : (i + 1) * rows, cols:].astype(jnp.bfloat16)


def far_sum(mine, theirs, rows, cols):
    count, depth = mine.shape
    return pl.pallas_call(
        functools.partial(far_sum_kernel, rows, cols),
        out_shape=[jax.ShapeDtypeStruct((count, cols), jnp.bfloat16)]
        + [jax.ShapeDtypeStruct((rows, depth - cols), jnp.bfloat16)] * (count // rows),
        in_specs=[VM] * 2,
        out_specs=[VM] * (count // rows + 1),
        compiler_params=pltpu.CompilerParams(vmem_limit_bytes=VMEM_LIMIT),
        name="far_sum",
    )(mine, theirs)


def near_sum_kernel(mine, theirs, stream, far, partial, own):
    rows, cols = mine.shape[0], partial.shape[1]
    total = mine[...].astype(jnp.float32) + theirs[...].astype(jnp.float32) + stream[0].astype(jnp.float32)
    partial[:rows, :] = total[:, :cols].astype(jnp.bfloat16)
    partial[rows:, :] = far[...]
    own[...] = total[:, cols:]


def near_sum(mine, theirs, stream, far):
    rows, depth = mine.shape
    count, cols = far.shape
    return pl.pallas_call(
        near_sum_kernel,
        out_shape=[
            jax.ShapeDtypeStruct((rows + count, cols), jnp.bfloat16),
            jax.ShapeDtypeStruct((rows, depth - cols), jnp.float32),
        ],
        in_specs=[VM] * 4,
        out_specs=[VM] * 2,
        compiler_params=pltpu.CompilerParams(vmem_limit_bytes=SMALL_LIMIT),
        name="near_sum",
    )(mine, theirs, stream, far)


def settle_kernel(x, after, out):
    out[...] = x[...]


def settle(x, after):
    return pl.pallas_call(
        settle_kernel,
        out_shape=jax.ShapeDtypeStruct(x.shape, x.dtype),
        in_specs=[VM, ANY],
        out_specs=VM,
        compiler_params=pltpu.CompilerParams(vmem_limit_bytes=SMALL_LIMIT),
        name="settle",
    )(x, after)


def join_kernel(rows, spare, mine, *refs):
    others, out = refs[: -1 - spare], refs[-1]
    for i in range(mine.shape[0] // rows):
        total = mine[i * rows : (i + 1) * rows, :].astype(jnp.float32)
        for k, other in enumerate(others):
            at = i ^ (k + 1)
            total = total + other[at * rows : (at + 1) * rows, :].astype(jnp.float32)
        out[i * rows : (i + 1) * rows, :] = total.astype(jnp.bfloat16)


def join(rows, mine, others, after):
    return pl.pallas_call(
        functools.partial(join_kernel, rows, len(after)),
        out_shape=jax.ShapeDtypeStruct(mine.shape, mine.dtype),
        in_specs=[VM] * (1 + len(others)) + [ANY] * len(after),
        out_specs=VM,
        compiler_params=pltpu.CompilerParams(vmem_limit_bytes=SMALL_LIMIT),
        name="join_chips",
    )(mine, *others, *after)


def project_rows_kernel(count, *refs):
    blocks, (gain, weight, total, squares, scaled) = refs[:count], refs[count:]
    rows, cols = blocks[0].shape
    here = slice(weight.shape[1] - cols, weight.shape[1])
    for i, block in enumerate(blocks):
        x = block[...].astype(jnp.float32)
        at = slice(i * rows, (i + 1) * rows)
        squares[at, :] = jnp.sum(x * x, axis=-1, keepdims=True)
        scaled[at, :] = (x * gain[:, here]).astype(jnp.bfloat16)
    total[...] = jnp.dot(scaled[...], weight[0, here, :], preferred_element_type=jnp.float32)


def project_rows(blocks, gain, weight):
    count = len(blocks)
    rows, cols = blocks[0].shape
    width = weight.shape[2]
    return pl.pallas_call(
        functools.partial(project_rows_kernel, count),
        out_shape=[
            jax.ShapeDtypeStruct((count * rows, width), jnp.float32),
            jax.ShapeDtypeStruct((count * rows, 1), jnp.float32),
        ],
        in_specs=[VM] * (count + 2),
        out_specs=[VM, VM],
        scratch_shapes=[pltpu.VMEM((count * rows, cols), jnp.bfloat16)],
        compiler_params=pltpu.CompilerParams(vmem_limit_bytes=VMEM_LIMIT),
        cost_estimate=pl.CostEstimate(
            flops=2 * count * rows * cols * width, bytes_accessed=2 * cols * width, transcendentals=0
        ),
        name="project_rows",
    )(*blocks, gain, weight)


def project_even_kernel(even, gain, weight, total, squares):
    cols = even.shape[1]
    x = even[...].astype(jnp.float32)
    squares[...] = jnp.sum(x * x, axis=-1, keepdims=True)
    scaled = (x * gain[:, :cols]).astype(jnp.bfloat16)
    total[...] = jnp.dot(scaled, weight[0, :cols, :], preferred_element_type=jnp.float32)


def project_even(even, gain, weight):
    count, cols = even.shape
    width = weight.shape[2]
    return pl.pallas_call(
        project_even_kernel,
        out_shape=[
            jax.ShapeDtypeStruct((count, width), jnp.float32),
            jax.ShapeDtypeStruct((count, 1), jnp.float32),
        ],
        in_specs=[VM] * 3,
        out_specs=[VM, VM],
        compiler_params=pltpu.CompilerParams(vmem_limit_bytes=VMEM_LIMIT),
        cost_estimate=pl.CostEstimate(
            flops=2 * count * cols * width, bytes_accessed=2 * cols * width, transcendentals=0
        ),
        name="project_even",
    )(even, gain, weight)


def project_odd_kernel(tile, odd, even, rest, gain, weight, *refs):
    near, near_squares, far, far_squares, even_total, even_squares, kept, out, made, sems = refs
    rows, cols = rest.shape[0], odd.shape[1]
    depth, width = weight.shape[1:]
    me = lax.axis_index("seq")
    copies = [
        pltpu.make_async_copy(even.at[:rows], kept.at[0, :, pl.ds(0, cols)], sems.at[0]),
        pltpu.make_async_copy(rest, kept.at[0, :, pl.ds(cols, depth - cols)], sems.at[1]),
    ]
    for c in copies:
        c.start()
    x = odd[...].astype(jnp.float32)
    odd_squares = jnp.sum(x * x, axis=-1, keepdims=True)
    scaled = (x * gain[:, :cols]).astype(jnp.bfloat16)
    places, scales = [], []
    for j in range(2 * odd.shape[0] // rows):
        at = pl.ds(pl.multiple_of((me ^ j) * rows, rows), rows)
        part = slice(j // 2 * rows, (j // 2 + 1) * rows)
        total, squares = (near, near_squares) if j < 2 else (far, far_squares)
        here = slice(j % 2 * rows, (j % 2 + 1) * rows) if j < 2 else slice((j - 2) * rows, (j - 1) * rows)
        mine = odd_squares[part] if j % 2 else even_squares[part, :]
        places.append((at, part, total, here))
        scales.append(lax.rsqrt((squares[here, :] + mine) / depth + 1e-06))
    for i in range(width // tile):
        lanes = pl.ds(i * tile, tile)
        product = jnp.dot(scaled, weight[0, :cols, lanes], preferred_element_type=jnp.float32)
        for j, (at, part, total, here) in enumerate(places):
            mine = product[part] if j % 2 else even_total[part, lanes]
            made[at, lanes] = ((total[here, lanes] + mine) * scales[j]).astype(jnp.bfloat16)
        copies.append(pltpu.make_async_copy(made.at[:, lanes], out.at[0, :, lanes], sems.at[2 + i]))
        copies[-1].start()
    for c in copies:
        c.wait()


def project_odd(n, odd, even, rest, gain, weight, near, far, evens):
    rows = rest.shape[0]
    _, depth, width = weight.shape
    tile = 256 if width % 256 == 0 else 128
    return pl.pallas_call(
        functools.partial(project_odd_kernel, tile),
        out_shape=[
            jax.ShapeDtypeStruct((1, rows, depth), jnp.bfloat16),
            jax.ShapeDtypeStruct((1, n * rows, width), jnp.bfloat16),
        ],
        in_specs=[VM] * 11,
        out_specs=[ANY, ANY],
        scratch_shapes=[
            pltpu.VMEM((n * rows, width), jnp.bfloat16),
            pltpu.SemaphoreType.DMA((2 + width // tile,)),
        ],
        compiler_params=pltpu.CompilerParams(vmem_limit_bytes=VMEM_LIMIT),
        cost_estimate=pl.CostEstimate(
            flops=n * rows * odd.shape[1] * width, bytes_accessed=2 * odd.shape[1] * width, transcendentals=0
        ),
        name="project_odd",
    )(odd, even, rest, gain, weight, *near, *far, *evens)


def mask_kernel(rows, mask, order, out):
    tokens = out.shape[0]
    windows, per, _ = mask.shape
    lanes = max(windows * per, 128)
    me = lax.axis_index("seq")
    row = lax.broadcasted_iota(jnp.int32, (tokens, tokens), 0)
    token = ((row // rows) ^ me) * rows + row % rows
    at = (order[...].reshape(1, tokens) == token).astype(jnp.bfloat16)
    position = lax.broadcasted_iota(jnp.int32, (tokens, lanes), 0)
    lane = lax.broadcasted_iota(jnp.int32, (tokens, lanes), 1)
    block = jnp.dot(
        at, (position // BLOCK == lane).astype(jnp.bfloat16), preferred_element_type=jnp.float32
    ).astype(jnp.bfloat16)
    first = lax.broadcasted_iota(jnp.int32, (lanes, lanes), 0)
    second = lax.broadcasted_iota(jnp.int32, (lanes, lanes), 1)
    visible = jnp.zeros((lanes, lanes), jnp.int32)
    for w in range(windows):
        for i in range(per):
            for j in range(per):
                here = (first == w * per + i) & (second == w * per + j)
                visible = jnp.where(here, mask[w, i, j], visible)
    visible = (visible > 0).astype(jnp.bfloat16)
    reach = jnp.dot(block, visible, preferred_element_type=jnp.float32).astype(jnp.bfloat16)
    seen = lax.dot_general(reach, block, (((1,), (1,)), ((), ())), preferred_element_type=jnp.float32)
    out[...] = jnp.where(seen > 0.5, 0.0, NEG)


def mask_bias(block_mask, token_order, n, rows):
    tokens = n * rows
    return pl.pallas_call(
        functools.partial(mask_kernel, rows),
        out_shape=jax.ShapeDtypeStruct((tokens, tokens), jnp.float32),
        in_specs=[pl.BlockSpec(memory_space=pltpu.SMEM), VM],
        out_specs=VM,
        compiler_params=pltpu.CompilerParams(vmem_limit_bytes=SMALL_LIMIT + 24 * tokens * tokens),
        name="mask_bias",
    )(block_mask, token_order)


def local(projected, stream_before, out_weight, proj_weight, norm_gain, block_mask, token_order):
    n = lax.axis_size("seq")
    rows = projected.shape[1]
    far_cut = cut(projected, n, tuple(range(2, n)))
    far = [swap(far_cut[j - 2], j) for j in range(2, n)]
    near_cut = cut(projected, n, (0, 1), (far_cut[-1],))
    blocks = [near_cut[0], swap(near_cut[1], 1)] + far
    stream, out_weight = load((stream_before, out_weight), (1, 4))
    bias = mask_bias(block_mask, token_order, n, rows)
    (proj_weight,) = load((proj_weight,), (8,), (out_weight,))
    bias, proj_weight = lax.optimization_barrier((bias, proj_weight))
    near_out, far_out = attend(blocks, bias, tuple(range(1, n, 2)), out_weight)
    near_own, far_own = attend(blocks, bias, tuple(range(0, n, 2)), out_weight)
    cols = out_weight.shape[2] * 7 // 16
    far_partial, *others = far_sum(far_own, swap(far_out, 1), rows, cols)
    partial, own = near_sum(near_own, swap(near_out, 1), stream, far_partial)
    partial = onward(partial, 0)
    total = own
    for k, x in enumerate(others):
        total = total + swap(x, 2 * k + 2).astype(jnp.float32)
    total = total.astype(jnp.bfloat16)
    rest = [onward(total, j) for j in range(0, n, 2)]
    partial = settle(partial, total)
    swapped = [swap(partial, j) for j in range(2, n, 2)]
    rest = [r for x in rest for r in (x, swap(x, 1))]
    far_total = project_rows(rest[2:], norm_gain, proj_weight)
    even = join(rows, partial, swapped, (*far_total, *rest[:2]))
    odd = swap(even, 1)
    near_total = project_rows(rest[:2], norm_gain, proj_weight)
    even_total = project_even(even, norm_gain, proj_weight)
    return project_odd(n, odd, even, rest[0], norm_gain, proj_weight, near_total, far_total, even_total)


def solution(mesh):
    placed = (
        P("segment", "seq", None),
        P("segment", "seq", None),
        P("segment", "seq", None),
        P("segment", None, "seq"),
        P("segment", None),
        P(),
        P(),
    )
    return jax.shard_map(
        local,
        mesh=mesh,
        in_specs=placed,
        out_specs=(P("segment", "seq", None), P("segment", None, "seq")),
        check_vma=False,
    )
```
